32 devices in a mesh: groups: 2 (over y), vocab: 4 (over z), rows: 2 (over x), teach: 2 (over core).
Axes of the slice: x: 2, y: 2, z: 4, core: 2. Of those that a mesh axis runs over, the one named last changes fastest.
Arguments:
- hidden_rows: bfloat16 [32, 3584], P(('groups', 'vocab')), parts along dimension 0, may hold values from -512 to 512
- mentor_unnormalized: float32 [32, 4864], P(('groups', 'teach'), ('vocab', 'rows')), parts along dimension 0, may hold values from -1000 to 1000
- head_weight: bfloat16 [4864, 3584], P(('vocab', 'rows', 'teach')), may hold values from -2 to 2
- row_mask: int32 [32], P('groups'), parts along dimension 0, may hold values 0 or 1
Outputs:
- divergence: float32 [32], P('groups'), parts along dimension 0
- hidden_grad: bfloat16 [32, 3584], P(('groups', 'vocab', 'rows', 'teach')), parts along dimension 0
- weight_grad: bfloat16 [9728, 3584], P(('groups', 'vocab', 'rows', 'teach')), parts along dimension 0
The draws below stay inside these ranges and needn't reach their ends.
There are 2 independent parts, one for each index of `groups`. The reference program is written for one: setup_inputs(seed, part) draws one part's arguments, and reference() takes and returns one part's arrays. A program takes and returns all parts, laid end to end along the dimension named above; an argument that names none is the same for every part. Nothing has to cross between parts.
All inputs are finite; a program needn't handle non-finite values.
Results may differ from the reference program's by a relative error of at most 0.0051.
Values may be sent and summed in bfloat16 or wider, within the bound.
A program may use at most 64 MiB of HBM per device.

```python
import math
import jax
import jax.numpy as jnp

D = 3584
V = 4864
ROWS = 16


def draw_hidden_rows(key, part):
    first, second = jax.random.split(key, 2)
    scales = jnp.exp(jax.random.uniform(second, (ROWS, 1), jnp.float32, math.log(0.3), math.log(3.0)))
    result = jnp.clip(jax.random.normal(first, (ROWS, D), jnp.float32), -4.0, 4.0) * scales
    return result.astype(jnp.bfloat16)


def draw_mentor_unnormalized(key, part):
    first = jax.random.fold_in(key, 0)
    position = jnp.arange(V).astype(jnp.float32)[None, :] / V
    ramp = 2.0 * jnp.log(1.0 + 2.0 * position)
    values = jnp.clip(jax.random.normal(first, (ROWS, V), jnp.float32), -4.0, 4.0)
    result = 4.0 * values + ramp
    return result.astype(jnp.float32)


def draw_head_weight(key, part):
    first = jax.random.fold_in(key, 0)
    weight_scale = 3.0 / math.sqrt(D)
    values = jnp.clip(jax.random.normal(first, (V, D), jnp.float32), -4.0, 4.0)
    return (values * weight_scale).astype(jnp.bfloat16)


def plant(entries, rng, smallest, largest):
    spot = [jax.random.randint(jax.random.fold_in(rng, axis), (), 0, length) for axis, length in enumerate(entries.shape)]
    main_axis = entries.shape.index(max(entries.shape))
    beside = spot[:main_axis] + [(spot[main_axis] + 1) % entries.shape[main_axis]] + spot[main_axis + 1:]
    return entries.at[tuple(spot)].set(smallest).at[tuple(beside)].set(largest)


def setup_inputs(seed: int = 0, part: int = 0) -> dict:
    streams_of = jax.random.split(jax.random.key(seed), 5)
    own_keys = jax.random.split(jax.random.fold_in(streams_of[4], part), 5)
    hidden_rows = draw_hidden_rows(jax.random.fold_in(jax.random.fold_in(streams_of[4], part), 71), part)
    mentor_unnormalized = draw_mentor_unnormalized(jax.random.fold_in(jax.random.fold_in(streams_of[4], part), 71), part)
    head_weight = draw_head_weight(jax.random.fold_in(streams_of[4], 71), part)
    row_mask = plant((jax.random.randint(own_keys[3], (ROWS,), 0, 4) < 3).astype(jnp.int32), jax.random.fold_in(own_keys[3], 1), 0, 1)
    return {"hidden_rows": hidden_rows, "mentor_unnormalized": mentor_unnormalized, "head_weight": head_weight, "row_mask": row_mask}


smoothing_divisor = 2.0
objective_scale = 256.0


def reference(hidden_rows, mentor_unnormalized, head_weight, row_mask):
    head_product_matrix = jnp.dot(hidden_rows, head_weight.T, preferred_element_type=jnp.float32)
    learner_unnormalized = head_product_matrix / smoothing_divisor
    divided_learner_values = mentor_unnormalized / smoothing_divisor
    max_student = jnp.max(learner_unnormalized, axis=1)
    sum_student = jnp.sum(jnp.exp(learner_unnormalized - max_student[:, None]), axis=1)
    lse_student = max_student + jnp.log(sum_student)
    max_teacher = jnp.max(divided_learner_values, axis=1)
    sum_teacher = jnp.sum(jnp.exp(divided_learner_values - max_teacher[:, None]), axis=1)
    lse_teacher = max_teacher + jnp.log(sum_teacher)
    mentor_softmax = jnp.exp(divided_learner_values - lse_teacher[:, None])
    learner_softmax = jnp.exp(learner_unnormalized - lse_student[:, None])
    valid_token_count = row_mask.astype(jnp.float32)
    divergence = valid_token_count * (jnp.sum(mentor_softmax * (divided_learner_values - learner_unnormalized), axis=1) - lse_teacher + lse_student)
    raw_score_derivative = (valid_token_count[:, None] * (objective_scale * smoothing_divisor) * (learner_softmax - mentor_softmax)).astype(jnp.bfloat16)
    hidden_grad = jnp.dot(raw_score_derivative, head_weight, preferred_element_type=jnp.float32).astype(jnp.bfloat16)
    weight_grad = jnp.dot(raw_score_derivative.T, hidden_rows, preferred_element_type=jnp.float32).astype(jnp.bfloat16)
    return (divergence, hidden_grad, weight_grad)
```

```python
import functools

import jax
import jax.numpy as jnp
from jax import lax
from jax.experimental import pallas as pl
from jax.experimental.pallas import tpu as pltpu
from jax.sharding import PartitionSpec as P

smoothing_divisor = 2.0
objective_scale = 256.0

LANES = 128
PACK = 16
CHUNK = 256


def dot(a, b, contract):
    return lax.dot_general(a, b, ((contract[:1], contract[1:]), ((), ())), preferred_element_type=jnp.float32)


def column_to_row(columns, width):
    rows = columns[0].shape[0]
    lane = lax.broadcasted_iota(jnp.int32, (rows, width), 1)
    row = lax.broadcasted_iota(jnp.int32, (rows, width), 0)
    total = jnp.zeros((rows, width), jnp.float32)
    for place, column in enumerate(columns):
        total = jnp.where(lane == row + place * rows, column, total)
    return jnp.sum(total, axis=0, keepdims=True)


def row_to_column(line, place, rows):
    width = line.shape[1]
    lane = lax.broadcasted_iota(jnp.int32, (rows, width), 1)
    row = lax.broadcasted_iota(jnp.int32, (rows, width), 0)
    return jnp.sum(jnp.where(lane == row + place * rows, line, 0.0), axis=1, keepdims=True)


def main_kernel(
    sizes,
    hid, mentor, w_hbm, mask,
    wg, hg, div,
    w, hsend, hrecv, h, tsend, trecv, ssend, srecv, part, gsend, grecv,
    w_sem, hs_sem, hr_sem, ts_sem, tr_sem, ss_sem, sr_sem, gs_sem, gr_sem,
):
    nz, nx, nc = sizes
    n = nz * nx * nc
    own, depth = hid.shape
    rows = own * nz
    vocab = w.shape[0]
    fold = PACK // own
    span = depth // fold
    chunks = depth // CHUNK
    half = mentor.shape[0]
    unroll = n <= 16

    z, x, c = lax.axis_index("vocab"), lax.axis_index("rows"), lax.axis_index("teach")
    me = (z * nx + x) * nc + c

    def place(index):
        return {
            "vocab": lax.div(index, nx * nc),
            "rows": lax.rem(lax.div(index, nc), nx),
            "teach": lax.rem(index, nc),
        }

    def others(step):
        def run(offset, carry):
            step(lax.rem(me + offset, n))
            return carry

        lax.fori_loop(1, n, run, 0, unroll=unroll)

    w_copy = pltpu.make_async_copy(w_hbm, w, w_sem)
    w_copy.start()

    barrier = pltpu.get_barrier_semaphore()
    others(
        lambda d: pl.semaphore_signal(
            barrier, inc=1, device_id=place(d), device_id_type=pl.DeviceIdType.MESH
        )
    )

    hidden = hid[...].astype(jnp.float32)
    packed = jnp.concatenate([hidden[:, k * span:(k + 1) * span] for k in range(fold)], axis=0).astype(jnp.bfloat16)
    hsend[...] = packed
    hrecv[z] = packed
    low = mentor[:, :vocab]
    high = mentor[:, vocab:2 * vocab]
    first = c == 0
    mine = jnp.where(first, low, high)
    tsend[:, :vocab] = jnp.where(first, high, low)
    part[...] = jnp.zeros_like(part)

    pl.semaphore_wait(barrier, n - 1)

    def hidden_copy(zz):
        return pltpu.make_async_remote_copy(
            src_ref=hsend, dst_ref=hrecv.at[z], send_sem=hs_sem, recv_sem=hr_sem,
            device_id={"vocab": zz}, device_id_type=pl.DeviceIdType.MESH,
        )

    def send_hidden(offset, carry):
        hidden_copy(lax.rem(z + offset, nz)).start()
        return carry

    lax.fori_loop(1, nz, send_hidden, 0, unroll=nz <= 4)
    teacher_copy = pltpu.make_async_remote_copy(
        src_ref=tsend, dst_ref=trecv, send_sem=ts_sem, recv_sem=tr_sem,
        device_id={"teach": 1 - c}, device_id_type=pl.DeviceIdType.MESH,
    )
    teacher_copy.start()

    teacher_copy.wait_recv()
    theirs = trecv[:, :vocab]
    scaled = jnp.concatenate(
        [jnp.where(first, mine, theirs), jnp.where(first, theirs, mine)], axis=0
    ) * (1.0 / smoothing_divisor)
    max_t = jnp.max(scaled, axis=1, keepdims=True)
    weight_t = jnp.exp(scaled - max_t)
    sum_t = jnp.sum(weight_t, axis=1, keepdims=True)

    w_copy.wait()
    pltpu.make_async_copy(hrecv.at[pl.ds(0, nz - 1)], hrecv.at[pl.ds(0, nz - 1)], hr_sem).wait()
    arrived = [hrecv[k].astype(jnp.float32) for k in range(nz)]
    for k in range(fold):
        h[:, k * span:(k + 1) * span] = jnp.concatenate(
            [a[k * own:(k + 1) * own] for a in arrived], axis=0
        ).astype(jnp.bfloat16)

    student = dot(h[...], w[...], (1, 1)) * (1.0 / smoothing_divisor)
    max_s = jnp.max(student, axis=1, keepdims=True)
    sum_s = jnp.sum(jnp.exp(student - max_s), axis=1, keepdims=True)
    cross = jnp.sum(weight_t * (scaled - student), axis=1, keepdims=True)

    width = ssend.shape[1]
    line = column_to_row([max_s, max_t, sum_s, sum_t, cross], width)
    ssend[...] = line
    srecv[me] = line

    def stat_copy(d):
        return pltpu.make_async_remote_copy(
            src_ref=ssend, dst_ref=srecv.at[me], send_sem=ss_sem, recv_sem=sr_sem,
            device_id=place(d), device_id_type=pl.DeviceIdType.MESH,
        )

    others(lambda d: stat_copy(d).start())
    pltpu.make_async_copy(srecv.at[pl.ds(0, n - 1)], srecv.at[pl.ds(0, n - 1)], sr_sem).wait()
    stats = srecv[:, 0, :]
    top = jnp.max(stats, axis=0, keepdims=True)
    scale = jnp.exp(stats - top)
    lane = lax.broadcasted_iota(jnp.int32, stats.shape, 1)
    scale = jnp.where(lane < 4 * rows, pltpu.roll(scale, 2 * rows, 1), pltpu.roll(scale, 3 * rows, 1))
    sums = jnp.sum(stats * scale, axis=0, keepdims=True)
    all_max_s, all_max_t = row_to_column(top, 0, rows), row_to_column(top, 1, rows)
    all_sum_s, all_sum_t, all_cross = (row_to_column(sums, k, rows) for k in (2, 3, 4))
    lse_s = all_max_s + jnp.log(all_sum_s)
    lse_t = all_max_t + jnp.log(all_sum_t)
    keep = row_to_column(mask[...].astype(jnp.float32), 0, rows)
    div[...] = column_to_row([keep * (all_cross / all_sum_t - lse_t + lse_s)], rows)

    grad = (
        keep * (objective_scale * smoothing_divisor) * (jnp.exp(student - lse_s) - jnp.exp(scaled - lse_t))
    ).astype(jnp.bfloat16)

    for k in range(chunks):
        term = dot(grad, w[:, k * CHUNK:(k + 1) * CHUNK], (1, 0))
        for q in range(0, CHUNK, LANES):
            part[q // LANES, pl.ds(k, rows, stride=PACK), :] = term[:, q:q + LANES]
    for q in range(0, CHUNK, LANES):
        gsend[:, :, q:q + LANES] = part[q // LANES].reshape(rows, PACK, LANES).astype(jnp.bfloat16)
    grecv[me] = gsend[me]

    def grad_copy(d):
        return pltpu.make_async_remote_copy(
            src_ref=gsend.at[d], dst_ref=grecv.at[me], send_sem=gs_sem, recv_sem=gr_sem,
            device_id=place(d), device_id_type=pl.DeviceIdType.MESH,
        )

    others(lambda d: grad_copy(d).start())

    for k in range(0, depth, 2 * CHUNK):
        wg[:, k:k + 2 * CHUNK] = dot(grad, h[:, k:k + 2 * CHUNK], (0, 0)).astype(jnp.bfloat16)

    pltpu.make_async_copy(grecv.at[pl.ds(0, n - 1)], grecv.at[pl.ds(0, n - 1)], gr_sem).wait()
    total = jnp.sum(grecv[...].astype(jnp.float32), axis=0)
    for k in range(chunks):
        hg[:, k * CHUNK:(k + 1) * CHUNK] = total[k:k + 1].astype(jnp.bfloat16)

    pltpu.make_async_copy(hrecv.at[pl.ds(0, nz - 1)], hrecv.at[pl.ds(0, nz - 1)], hs_sem).wait()
    teacher_copy.wait_send()
    pltpu.make_async_copy(srecv.at[pl.ds(0, n - 1)], srecv.at[pl.ds(0, n - 1)], ss_sem).wait()
    pltpu.make_async_copy(grecv.at[pl.ds(0, n - 1)], grecv.at[pl.ds(0, n - 1)], gs_sem).wait()


def body(sizes, hidden_rows, mentor_unnormalized, head_weight, row_mask):
    nz, nx, nc = sizes
    n = nz * nx * nc
    own, depth = hidden_rows.shape
    vocab = head_weight.shape[0]
    rows = own * nz
    half = mentor_unnormalized.shape[0]
    assert rows == n and nc == 2 and PACK % own == 0 and depth % (2 * CHUNK) == 0 and depth // CHUNK <= PACK
    fold = PACK // own
    wide = -(-vocab // LANES) * LANES
    width = -(-5 * rows // LANES) * LANES
    vmem = pl.BlockSpec(memory_space=pltpu.VMEM)
    dma = pltpu.SemaphoreType.DMA
    wg, hg, div = pl.pallas_call(
        functools.partial(main_kernel, sizes),
        out_shape=(
            jax.ShapeDtypeStruct((vocab, depth), jnp.bfloat16),
            jax.ShapeDtypeStruct((1, depth), jnp.bfloat16),
            jax.ShapeDtypeStruct((1, rows), jnp.float32),
        ),
        in_specs=[vmem, vmem, pl.BlockSpec(memory_space=pl.ANY), vmem],
        out_specs=(vmem, vmem, vmem),
        scratch_shapes=[
            pltpu.VMEM((vocab, depth), jnp.bfloat16),
            pltpu.VMEM((PACK, depth // fold), jnp.bfloat16),
            pltpu.VMEM((nz, PACK, depth // fold), jnp.bfloat16),
            pltpu.VMEM((rows, depth), jnp.bfloat16),
            pltpu.VMEM((half, wide), jnp.float32),
            pltpu.VMEM((half, wide), jnp.float32),
            pltpu.VMEM((1, width), jnp.float32),
            pltpu.VMEM((n, 1, width), jnp.float32),
            pltpu.VMEM((CHUNK // LANES, rows * PACK, LANES), jnp.float32),
            pltpu.VMEM((rows, PACK, CHUNK), jnp.bfloat16),
            pltpu.VMEM((n, PACK, CHUNK), jnp.bfloat16),
        ] + [dma] * 9,
        compiler_params=pltpu.CompilerParams(
            collective_id=0, has_side_effects=True, vmem_limit_bytes=44 * 2**20
        ),
    )(hidden_rows, mentor_unnormalized, head_weight, row_mask.reshape(1, rows))
    return div.reshape(rows), hg, wg


def solution(mesh):
    sizes = (mesh.shape["vocab"], mesh.shape["rows"], mesh.shape["teach"])
    return jax.shard_map(
        functools.partial(body, sizes),
        mesh=mesh,
        in_specs=(
            P(("groups", "vocab"), None),
            P(("groups", "teach"), ("vocab", "rows")),
            P(("vocab", "rows", "teach"), None),
            P("groups"),
        ),
        out_specs=(
            P("groups"),
            P(("groups", "vocab", "rows", "teach"), None),
            P(("groups", "vocab", "rows", "teach"), None),
        ),
        check_vma=False,
    )
```

```python
import functools

import jax
import jax.numpy as jnp
from jax import lax
from jax.experimental import pallas as pl
from jax.experimental.pallas import tpu as pltpu
from jax.sharding import PartitionSpec as P

smoothing_divisor = 2.0
objective_scale = 256.0

LANES = 128
PACK = 16


def dot(a, b, contract):
    return lax.dot_general(a, b, ((contract[:1], contract[1:]), ((), ())), preferred_element_type=jnp.float32)


def column_to_row(columns, width):
    rows = columns[0].shape[0]
    lane = lax.broadcasted_iota(jnp.int32, (rows, width), 1)
    row = lax.broadcasted_iota(jnp.int32, (rows, width), 0)
    total = jnp.zeros((rows, width), jnp.float32)
    for place, column in enumerate(columns):
        total = jnp.where(lane == row + place * rows, column, total)
    return jnp.sum(total, axis=0, keepdims=True)


def row_to_column(line, place, rows):
    width = line.shape[1]
    lane = lax.broadcasted_iota(jnp.int32, (rows, width), 1)
    row = lax.broadcasted_iota(jnp.int32, (rows, width), 0)
    return jnp.sum(jnp.where(lane == row + place * rows, line, 0.0), axis=1, keepdims=True)


def main_kernel(
    sizes,
    hid_hbm, mentor_hbm, w_hbm, mask_hbm,
    wg, hg, div,
    hid, mentor, mask, w, hsend, hrecv, h, tsend, trecv, ssend, srecv, part, gsend, grecv,
    hid_sem, mentor_sem, mask_sem, w_sem,
    hs_sem, hr_sem, ts_sem, tr_sem, ss_sem, sr_sem, gs_sem, gr_sem,
):
    nz, nx, nc = sizes
    n = nz * nx * nc
    own, depth = hid.shape
    rows = own * nz
    vocab = w.shape[0]
    fold = PACK // own
    span = depth // fold
    halves = part.shape[0]
    reach = depth // halves
    unrolled = n <= 16

    z, x, c = lax.axis_index("vocab"), lax.axis_index("rows"), lax.axis_index("teach")
    me = (z * nx + x) * nc + c

    inputs = [
        pltpu.make_async_copy(hid_hbm, hid, hid_sem),
        pltpu.make_async_copy(mentor_hbm, mentor, mentor_sem),
        pltpu.make_async_copy(mask_hbm, mask, mask_sem),
        pltpu.make_async_copy(w_hbm, w, w_sem),
    ]
    for copy in inputs:
        copy.start()

    def others(step):
        if unrolled:
            zs = [z] + [lax.rem(z + k, nz) for k in range(1, nz)]
            xs = [x] + [lax.rem(x + k, nx) for k in range(1, nx)]
            cs = [c] + [lax.rem(c + k, nc) for k in range(1, nc)]
            for i in reversed(range(1, n)):
                zz, xx, cc = zs[i // (nx * nc)], xs[i // nc % nx], cs[i % nc]
                step((zz * nx + xx) * nc + cc, {"vocab": zz, "rows": xx, "teach": cc})
            return

        def run(offset, carry):
            d = lax.rem(me + offset, n)
            step(d, {
                "vocab": lax.div(d, nx * nc), "rows": lax.rem(lax.div(d, nc), nx), "teach": lax.rem(d, nc),
            })
            return carry

        lax.fori_loop(1, n, run, 0)

    barrier = pltpu.get_barrier_semaphore()
    others(
        lambda d, at: pl.semaphore_signal(
            barrier, inc=1, device_id=at, device_id_type=pl.DeviceIdType.MESH
        )
    )

    inputs[0].wait()
    hidden = hid[...].astype(jnp.float32)
    packed = jnp.concatenate([hidden[:, k * span:(k + 1) * span] for k in range(fold)], axis=0).astype(jnp.bfloat16)
    hsend[...] = packed
    hrecv[z] = packed
    inputs[1].wait()
    low = mentor[:, :vocab]
    high = mentor[:, vocab:2 * vocab]
    first = c == 0
    mine = jnp.where(first, low, high)
    tsend[:, :vocab] = jnp.where(first, high, low)
    part[...] = jnp.zeros_like(part)
    inputs[2].wait()
    keep = row_to_column(mask[...].astype(jnp.float32), 0, rows)

    pl.semaphore_wait(barrier, n - 1)

    def send_hidden(offset, carry):
        pltpu.make_async_remote_copy(
            src_ref=hsend, dst_ref=hrecv.at[z], send_sem=hs_sem, recv_sem=hr_sem,
            device_id={"vocab": lax.rem(z + offset, nz)}, device_id_type=pl.DeviceIdType.MESH,
        ).start()
        return carry

    teacher_copy = pltpu.make_async_remote_copy(
        src_ref=tsend, dst_ref=trecv, send_sem=ts_sem, recv_sem=tr_sem,
        device_id={"teach": 1 - c}, device_id_type=pl.DeviceIdType.MESH,
    )
    teacher_copy.start()
    lax.fori_loop(1, nz, send_hidden, 0, unroll=nz <= 4)

    teacher_copy.wait_recv()
    theirs = trecv[:, :vocab]
    scaled = jnp.concatenate(
        [jnp.where(first, mine, theirs), jnp.where(first, theirs, mine)], axis=0
    ) * (1.0 / smoothing_divisor)
    max_t = jnp.max(scaled, axis=1, keepdims=True)
    weight_t = jnp.exp(scaled - max_t)
    sum_t = jnp.sum(weight_t, axis=1, keepdims=True)

    inputs[3].wait()
    pltpu.make_async_copy(hrecv.at[pl.ds(0, nz - 1)], hrecv.at[pl.ds(0, nz - 1)], hr_sem).wait()
    arrived = [hrecv[k].astype(jnp.float32) for k in range(nz)]
    for k in range(fold):
        h[:, k * span:(k + 1) * span] = jnp.concatenate(
            [a[k * own:(k + 1) * own] for a in arrived], axis=0
        ).astype(jnp.bfloat16)

    student = dot(h[...], w[...], (1, 1)) * (1.0 / smoothing_divisor)
    max_s = jnp.max(student, axis=1, keepdims=True)
    sum_s = jnp.sum(jnp.exp(student - max_s), axis=1, keepdims=True)
    cross = jnp.sum(weight_t * (scaled - student), axis=1, keepdims=True)

    width = ssend.shape[1]
    line = column_to_row([max_s, max_t, sum_s, sum_t, cross], width)
    ssend[...] = line
    srecv[me] = line
    others(
        lambda d, at: pltpu.make_async_remote_copy(
            src_ref=ssend, dst_ref=srecv.at[me], send_sem=ss_sem, recv_sem=sr_sem,
            device_id=at, device_id_type=pl.DeviceIdType.MESH,
        ).start()
    )
    pltpu.make_async_copy(srecv.at[pl.ds(0, n - 1)], srecv.at[pl.ds(0, n - 1)], sr_sem).wait()
    stats = srecv[:, 0, :]
    top = jnp.max(stats, axis=0, keepdims=True)
    scale = jnp.exp(stats - top)
    lane = lax.broadcasted_iota(jnp.int32, stats.shape, 1)
    scale = jnp.where(lane < 4 * rows, pltpu.roll(scale, 2 * rows, 1), pltpu.roll(scale, 3 * rows, 1))
    sums = jnp.sum(stats * scale, axis=0, keepdims=True)
    all_max_s, all_max_t = row_to_column(top, 0, rows), row_to_column(top, 1, rows)
    all_sum_s, all_sum_t, all_cross = (row_to_column(sums, k, rows) for k in (2, 3, 4))
    lse_s = all_max_s + jnp.log(all_sum_s)
    lse_t = all_max_t + jnp.log(all_sum_t)

    grad = (
        keep * (objective_scale * smoothing_divisor) * (jnp.exp(student - lse_s) - jnp.exp(scaled - lse_t))
    ).astype(jnp.bfloat16)

    for s in range(halves):
        term = dot(grad, w[:, s * reach:(s + 1) * reach], (1, 0))
        for k in range(reach // LANES):
            part[s, pl.ds(k, rows, stride=PACK), :] = term[:, k * LANES:(k + 1) * LANES]
        gsend[s] = part[s].reshape(rows, PACK, LANES).astype(jnp.bfloat16)
        others(
            lambda d, at: pltpu.make_async_remote_copy(
                src_ref=gsend.at[s, d], dst_ref=grecv.at[s, me], send_sem=gs_sem.at[s], recv_sem=gr_sem.at[s],
                device_id=at, device_id_type=pl.DeviceIdType.MESH,
            ).start()
        )
        grecv[s, me] = gsend[s, me]

    div[...] = column_to_row([keep * (all_cross / all_sum_t - lse_t + lse_s)], rows)
    step = depth // 7 if depth % (7 * LANES) == 0 else LANES
    for k in range(0, depth, step):
        wg[:, k:k + step] = dot(grad, h[:, k:k + step], (0, 0)).astype(jnp.bfloat16)

    for s in range(halves):
        rest = grecv.at[s, pl.ds(0, n - 1)]
        pltpu.make_async_copy(rest, rest, gr_sem.at[s]).wait()
        total = jnp.sum(grecv[s].astype(jnp.float32), axis=0)
        for k in range(reach // LANES):
            at = s * reach + k * LANES
            hg[:, at:at + LANES] = total[k:k + 1].astype(jnp.bfloat16)

    pltpu.make_async_copy(hrecv.at[pl.ds(0, nz - 1)], hrecv.at[pl.ds(0, nz - 1)], hs_sem).wait()
    teacher_copy.wait_send()
    pltpu.make_async_copy(srecv.at[pl.ds(0, n - 1)], srecv.at[pl.ds(0, n - 1)], ss_sem).wait()
    for s in range(halves):
        rest = grecv.at[s, pl.ds(0, n - 1)]
        pltpu.make_async_copy(rest, rest, gs_sem.at[s]).wait()


def write_kernel(wg, hg, div, wg_out, hg_out, div_out, wg_sem, hg_sem, div_sem):
    copies = [
        pltpu.make_async_copy(wg, wg_out, wg_sem),
        pltpu.make_async_copy(hg, hg_out, hg_sem),
        pltpu.make_async_copy(div, div_out, div_sem),
    ]
    for copy in copies:
        copy.start()
    for copy in copies:
        copy.wait()


def body(sizes, hidden_rows, mentor_unnormalized, head_weight, row_mask):
    nz, nx, nc = sizes
    n = nz * nx * nc
    own, depth = hidden_rows.shape
    vocab = head_weight.shape[0]
    rows = own * nz
    half = mentor_unnormalized.shape[0]
    assert rows == n and nc == 2 and PACK % own == 0
    fold = PACK // own
    halves = 2
    assert depth % (halves * LANES) == 0 and depth // (halves * LANES) <= PACK
    wide = -(-vocab // LANES) * LANES
    width = -(-5 * rows // LANES) * LANES
    vmem = pl.BlockSpec(memory_space=pltpu.VMEM)
    hbm = pl.BlockSpec(memory_space=pltpu.HBM)
    dma = pltpu.SemaphoreType.DMA
    results = (
        jax.ShapeDtypeStruct((vocab, depth), jnp.bfloat16),
        jax.ShapeDtypeStruct((1, depth), jnp.bfloat16),
        jax.ShapeDtypeStruct((1, rows), jnp.float32),
    )
    made = pl.pallas_call(
        functools.partial(main_kernel, sizes),
        out_shape=results,
        in_specs=[hbm, hbm, hbm, hbm],
        out_specs=(vmem, vmem, vmem),
        scratch_shapes=[
            pltpu.VMEM((own, depth), jnp.bfloat16),
            pltpu.VMEM(mentor_unnormalized.shape, jnp.float32),
            pltpu.VMEM((1, rows), jnp.int32),
            pltpu.VMEM((vocab, depth), jnp.bfloat16),
            pltpu.VMEM((PACK, depth // fold), jnp.bfloat16),
            pltpu.VMEM((nz, PACK, depth // fold), jnp.bfloat16),
            pltpu.VMEM((rows, depth), jnp.bfloat16),
            pltpu.VMEM((half, wide), jnp.float32),
            pltpu.VMEM((half, wide), jnp.float32),
            pltpu.VMEM((1, width), jnp.float32),
            pltpu.VMEM((n, 1, width), jnp.float32),
            pltpu.VMEM((halves, rows * PACK, LANES), jnp.float32),
            pltpu.VMEM((halves, rows, PACK, LANES), jnp.bfloat16),
            pltpu.VMEM((halves, n, PACK, LANES), jnp.bfloat16),
        ] + [dma] * 10 + [dma((halves,))] * 2,
        compiler_params=pltpu.CompilerParams(
            collective_id=0, has_side_effects=True, vmem_limit_bytes=44 * 2**20
        ),
    )(*(
        pltpu.with_memory_space_constraint(a, pltpu.HBM)
        for a in (hidden_rows, mentor_unnormalized, head_weight, row_mask.reshape(1, rows))
    ))
    wg, hg, div = pl.pallas_call(
        write_kernel,
        out_shape=results,
        in_specs=[vmem, vmem, vmem],
        out_specs=(hbm, hbm, hbm),
        scratch_shapes=[dma] * 3,
    )(*made)
    return div.reshape(rows), hg, wg


def solution(mesh):
    sizes = (mesh.shape["vocab"], mesh.shape["rows"], mesh.shape["teach"])
    return jax.shard_map(
        functools.partial(body, sizes),
        mesh=mesh,
        in_specs=(
            P(("groups", "vocab"), None),
            P(("groups", "teach"), ("vocab", "rows")),
            P(("vocab", "rows", "teach"), None),
            P("groups"),
        ),
        out_specs=(
            P("groups"),
            P(("groups", "vocab", "rows", "teach"), None),
            P(("groups", "vocab", "rows", "teach"), None),
        ),
        check_vma=False,
    )
```

```python
import functools

import jax
import jax.numpy as jnp
from jax import lax
from jax.experimental import pallas as pl
from jax.experimental.pallas import tpu as pltpu
from jax.sharding import PartitionSpec as P

smoothing_divisor = 2.0
objective_scale = 256.0

LANES = 128
PACK = 16


def dot(a, b, contract):
    return lax.dot_general(a, b, ((contract[:1], contract[1:]), ((), ())), preferred_element_type=jnp.float32)


def column_to_row(columns, width):
    rows = columns[0].shape[0]
    lane = lax.broadcasted_iota(jnp.int32, (rows, width), 1)
    row = lax.broadcasted_iota(jnp.int32, (rows, width), 0)
    total = jnp.zeros((rows, width), jnp.float32)
    for place, column in enumerate(columns):
        total = jnp.where(lane == row + place * rows, column, total)
    return jnp.sum(total, axis=0, keepdims=True)


def row_to_column(line, place, rows):
    width = line.shape[1]
    lane = lax.broadcasted_iota(jnp.int32, (rows, width), 1)
    row = lax.broadcasted_iota(jnp.int32, (rows, width), 0)
    return jnp.sum(jnp.where(lane == row + place * rows, line, 0.0), axis=1, keepdims=True)


def partners(index, size):
    if size & (size - 1):
        return [index] + [lax.rem(index + k, size) for k in range(1, size)]
    result = []
    for k in range(size):
        value = index
        for bit in range(size.bit_length() - 1):
            if k >> bit & 1:
                value = value + (1 - 2 * lax.rem(lax.div(index, 1 << bit), 2)) * (1 << bit)
        result.append(value)
    return result


def main_kernel(
    sizes,
    hid_hbm, mentor_hbm, w_hbm, mask_hbm,
    wg, hg, div,
    hid, mentor, mask, w, hsend, hrecv, h, tsend, trecv, ssend, srecv, part, gsend, grecv,
    hid_sem, mentor_sem, mask_sem, w_sem,
    hs_sem, hr_sem, ts_sem, tr_sem, ss_sem, sr_sem, gs_sem, gr_sem,
):
    nz, nx, nc = sizes
    n = nz * nx * nc
    own, depth = hid.shape
    rows = own * nz
    vocab = w.shape[0]
    fold = PACK // own
    span = depth // fold
    halves = part.shape[0]
    reach = depth // halves
    unrolled = n <= 16

    z, x, c = lax.axis_index("vocab"), lax.axis_index("rows"), lax.axis_index("teach")
    me = (z * nx + x) * nc + c

    inputs = [
        pltpu.make_async_copy(hid_hbm, hid, hid_sem),
        pltpu.make_async_copy(mentor_hbm, mentor, mentor_sem),
        pltpu.make_async_copy(mask_hbm, mask, mask_sem),
        pltpu.make_async_copy(w_hbm, w, w_sem),
    ]
    for copy in inputs:
        copy.start()

    def others(step):
        if unrolled:
            zs, xs, cs = partners(z, nz), partners(x, nx), partners(c, nc)
            for i in reversed(range(1, n)):
                zz, xx, cc = zs[i // (nx * nc)], xs[i // nc % nx], cs[i % nc]
                step((zz * nx + xx) * nc + cc, {"vocab": zz, "rows": xx, "teach": cc})
            return

        def run(offset, carry):
            d = lax.rem(me + offset, n)
            step(d, {
                "vocab": lax.div(d, nx * nc), "rows": lax.rem(lax.div(d, nc), nx), "teach": lax.rem(d, nc),
            })
            return carry

        lax.fori_loop(1, n, run, 0)

    barrier = pltpu.get_barrier_semaphore()
    others(
        lambda d, at: pl.semaphore_signal(
            barrier, inc=1, device_id=at, device_id_type=pl.DeviceIdType.MESH
        )
    )

    inputs[0].wait()
    hidden = hid[...].astype(jnp.float32)
    packed = jnp.concatenate([hidden[:, k * span:(k + 1) * span] for k in range(fold)], axis=0).astype(jnp.bfloat16)
    hsend[...] = packed
    hrecv[z] = packed
    inputs[1].wait()
    low = mentor[:, :vocab]
    high = mentor[:, vocab:2 * vocab]
    first = c == 0
    mine = jnp.where(first, low, high)
    tsend[:, :vocab] = jnp.where(first, high, low)
    part[...] = jnp.zeros_like(part)
    inputs[2].wait()
    keep = row_to_column(mask[...].astype(jnp.float32), 0, rows)

    pl.semaphore_wait(barrier, n - 1)

    def send_hidden(offset, carry):
        pltpu.make_async_remote_copy(
            src_ref=hsend, dst_ref=hrecv.at[z], send_sem=hs_sem, recv_sem=hr_sem,
            device_id={"vocab": lax.rem(z + offset, nz)}, device_id_type=pl.DeviceIdType.MESH,
        ).start()
        return carry

    teacher_copy = pltpu.make_async_remote_copy(
        src_ref=tsend, dst_ref=trecv, send_sem=ts_sem, recv_sem=tr_sem,
        device_id={"teach": 1 - c}, device_id_type=pl.DeviceIdType.MESH,
    )
    teacher_copy.start()
    lax.fori_loop(1, nz, send_hidden, 0, unroll=nz <= 4)

    teacher_copy.wait_recv()
    theirs = trecv[:, :vocab]
    scaled = jnp.concatenate(
        [jnp.where(first, mine, theirs), jnp.where(first, theirs, mine)], axis=0
    ) * (1.0 / smoothing_divisor)
    max_t = jnp.max(scaled, axis=1, keepdims=True)
    weight_t = jnp.exp(scaled - max_t)
    sum_t = jnp.sum(weight_t, axis=1, keepdims=True)

    inputs[3].wait()
    pltpu.make_async_copy(hrecv.at[pl.ds(0, nz - 1)], hrecv.at[pl.ds(0, nz - 1)], hr_sem).wait()
    arrived = [hrecv[k].astype(jnp.float32) for k in range(nz)]
    for k in range(fold):
        h[:, k * span:(k + 1) * span] = jnp.concatenate(
            [a[k * own:(k + 1) * own] for a in arrived], axis=0
        ).astype(jnp.bfloat16)

    student = dot(h[...], w[...], (1, 1)) * (1.0 / smoothing_divisor)
    max_s = jnp.max(student, axis=1, keepdims=True)
    sum_s = jnp.sum(jnp.exp(student - max_s), axis=1, keepdims=True)
    cross = jnp.sum(weight_t * (scaled - student), axis=1, keepdims=True)

    width = ssend.shape[1]
    line = column_to_row([max_s, max_t, sum_s, sum_t, cross], width)
    ssend[...] = line
    srecv[me] = line
    others(
        lambda d, at: pltpu.make_async_remote_copy(
            src_ref=ssend, dst_ref=srecv.at[me], send_sem=ss_sem, recv_sem=sr_sem,
            device_id=at, device_id_type=pl.DeviceIdType.MESH,
        ).start()
    )
    pltpu.make_async_copy(srecv.at[pl.ds(0, n - 1)], srecv.at[pl.ds(0, n - 1)], sr_sem).wait()
    stats = srecv[:, 0, :]
    top = jnp.max(stats, axis=0, keepdims=True)
    scale = jnp.exp(stats - top)
    lane = lax.broadcasted_iota(jnp.int32, stats.shape, 1)
    scale = jnp.where(lane < 4 * rows, pltpu.roll(scale, 2 * rows, 1), pltpu.roll(scale, 3 * rows, 1))
    sums = jnp.sum(stats * scale, axis=0, keepdims=True)
    all_max_s, all_max_t = row_to_column(top, 0, rows), row_to_column(top, 1, rows)
    all_sum_s, all_sum_t, all_cross = (row_to_column(sums, k, rows) for k in (2, 3, 4))
    lse_s = all_max_s + jnp.log(all_sum_s)
    lse_t = all_max_t + jnp.log(all_sum_t)

    grad = (
        keep * (objective_scale * smoothing_divisor) * (jnp.exp(student - lse_s) - jnp.exp(scaled - lse_t))
    ).astype(jnp.bfloat16)

    for s in range(halves):
        term = dot(grad, w[:, s * reach:(s + 1) * reach], (1, 0))
        for k in range(reach // LANES):
            part[s, pl.ds(k, rows, stride=PACK), :] = term[:, k * LANES:(k + 1) * LANES]
        gsend[s] = part[s].reshape(rows, PACK, LANES).astype(jnp.bfloat16)
        others(
            lambda d, at: pltpu.make_async_remote_copy(
                src_ref=gsend.at[s, d], dst_ref=grecv.at[s, me], send_sem=gs_sem.at[s], recv_sem=gr_sem.at[s],
                device_id=at, device_id_type=pl.DeviceIdType.MESH,
            ).start()
        )
        grecv[s, me] = gsend[s, me]

    div[...] = column_to_row([keep * (all_cross / all_sum_t - lse_t + lse_s)], rows)
    step = depth // 7 if depth % (7 * LANES) == 0 else LANES
    for k in range(0, depth, step):
        wg[:, k:k + step] = dot(grad, h[:, k:k + step], (0, 0)).astype(jnp.bfloat16)

    for s in range(halves):
        rest = grecv.at[s, pl.ds(0, n - 1)]
        pltpu.make_async_copy(rest, rest, gr_sem.at[s]).wait()
        total = jnp.sum(grecv[s].astype(jnp.float32), axis=0)
        for k in range(reach // LANES):
            at = s * reach + k * LANES
            hg[:, at:at + LANES] = total[k:k + 1].astype(jnp.bfloat16)

    pltpu.make_async_copy(hrecv.at[pl.ds(0, nz - 1)], hrecv.at[pl.ds(0, nz - 1)], hs_sem).wait()
    teacher_copy.wait_send()
    pltpu.make_async_copy(srecv.at[pl.ds(0, n - 1)], srecv.at[pl.ds(0, n - 1)], ss_sem).wait()
    for s in range(halves):
        rest = grecv.at[s, pl.ds(0, n - 1)]
        pltpu.make_async_copy(rest, rest, gs_sem.at[s]).wait()


def write_kernel(wg, hg, div, wg_out, hg_out, div_out, wg_sem, hg_sem, div_sem):
    vocab = wg.shape[0]
    slab = -(-vocab // (wg_sem.shape[0] * PACK)) * PACK
    copies = [pltpu.make_async_copy(hg, hg_out, hg_sem), pltpu.make_async_copy(div, div_out, div_sem)]
    for k, first in enumerate(range(0, vocab, slab)):
        at = pl.ds(first, min(slab, vocab - first))
        copies.append(pltpu.make_async_copy(wg.at[at], wg_out.at[at], wg_sem.at[k]))
    for copy in copies:
        copy.start()
    for copy in copies:
        copy.wait()


def body(sizes, hidden_rows, mentor_unnormalized, head_weight, row_mask):
    nz, nx, nc = sizes
    n = nz * nx * nc
    own, depth = hidden_rows.shape
    vocab = head_weight.shape[0]
    rows = own * nz
    half = mentor_unnormalized.shape[0]
    assert rows == n and nc == 2 and PACK % own == 0
    fold = PACK // own
    halves = 2
    assert depth % (halves * LANES) == 0 and depth // (halves * LANES) <= PACK
    wide = -(-vocab // LANES) * LANES
    width = -(-5 * rows // LANES) * LANES
    vmem = pl.BlockSpec(memory_space=pltpu.VMEM)
    hbm = pl.BlockSpec(memory_space=pltpu.HBM)
    dma = pltpu.SemaphoreType.DMA
    results = (
        jax.ShapeDtypeStruct((vocab, depth), jnp.bfloat16),
        jax.ShapeDtypeStruct((1, depth), jnp.bfloat16),
        jax.ShapeDtypeStruct((1, rows), jnp.float32),
    )
    made = pl.pallas_call(
        functools.partial(main_kernel, sizes),
        out_shape=results,
        in_specs=[hbm, hbm, hbm, hbm],
        out_specs=(vmem, vmem, vmem),
        scratch_shapes=[
            pltpu.VMEM((own, depth), jnp.bfloat16),
            pltpu.VMEM(mentor_unnormalized.shape, jnp.float32),
            pltpu.VMEM((1, rows), jnp.int32),
            pltpu.VMEM((vocab, depth), jnp.bfloat16),
            pltpu.VMEM((PACK, depth // fold), jnp.bfloat16),
            pltpu.VMEM((nz, PACK, depth // fold), jnp.bfloat16),
            pltpu.VMEM((rows, depth), jnp.bfloat16),
            pltpu.VMEM((half, wide), jnp.float32),
            pltpu.VMEM((half, wide), jnp.float32),
            pltpu.VMEM((1, width), jnp.float32),
            pltpu.VMEM((n, 1, width), jnp.float32),
            pltpu.VMEM((halves, rows * PACK, LANES), jnp.float32),
            pltpu.VMEM((halves, rows, PACK, LANES), jnp.bfloat16),
            pltpu.VMEM((halves, n, PACK, LANES), jnp.bfloat16),
        ] + [dma] * 10 + [dma((halves,))] * 2,
        compiler_params=pltpu.CompilerParams(
            collective_id=0, has_side_effects=True, vmem_limit_bytes=44 * 2**20
        ),
    )(*(
        pltpu.with_memory_space_constraint(a, pltpu.HBM)
        for a in (hidden_rows, mentor_unnormalized, head_weight, row_mask.reshape(1, rows))
    ))
    wg, hg, div = pl.pallas_call(
        write_kernel,
        out_shape=results,
        in_specs=[vmem, vmem, vmem],
        out_specs=(hbm, hbm, hbm),
        scratch_shapes=[dma((4,)), dma, dma],
        compiler_params=pltpu.CompilerParams(vmem_limit_bytes=4 * 2**20),
    )(*(pltpu.with_memory_space_constraint(a, pltpu.VMEM) for a in made))
    return div.reshape(rows), hg, wg


def solution(mesh):
    sizes = (mesh.shape["vocab"], mesh.shape["rows"], mesh.shape["teach"])
    return jax.shard_map(
        functools.partial(body, sizes),
        mesh=mesh,
        in_specs=(
            P(("groups", "vocab"), None),
            P(("groups", "teach"), ("vocab", "rows")),
            P(("vocab", "rows", "teach"), None),
            P("groups"),
        ),
        out_specs=(
            P("groups"),
            P(("groups", "vocab", "rows", "teach"), None),
            P(("groups", "vocab", "rows", "teach"), None),
        ),
        check_vma=False,
    )
```

```python
import functools

import jax
import jax.numpy as jnp
from jax import lax
from jax.experimental import pallas as pl
from jax.experimental.pallas import tpu as pltpu
from jax.sharding import PartitionSpec as P

smoothing_divisor = 2.0
objective_scale = 256.0

LANES = 128
PACK = 16


def dot(a, b, contract):
    return lax.dot_general(a, b, ((contract[:1], contract[1:]), ((), ())), preferred_element_type=jnp.float32)


def column_to_row(columns, width):
    rows = columns[0].shape[0]
    lane = lax.broadcasted_iota(jnp.int32, (rows, width), 1)
    row = lax.broadcasted_iota(jnp.int32, (rows, width), 0)
    total = jnp.zeros((rows, width), jnp.float32)
    for place, column in enumerate(columns):
        total = jnp.where(lane == row + place * rows, column, total)
    return jnp.sum(total, axis=0, keepdims=True)


def row_to_column(line, place, rows):
    width = line.shape[1]
    lane = lax.broadcasted_iota(jnp.int32, (rows, width), 1)
    row = lax.broadcasted_iota(jnp.int32, (rows, width), 0)
    return jnp.sum(jnp.where(lane == row + place * rows, line, 0.0), axis=1, keepdims=True)


def partners(index, size):
    if size & (size - 1):
        return [index] + [lax.rem(index + k, size) for k in range(1, size)]
    result = []
    for k in range(size):
        value = index
        for bit in range(size.bit_length() - 1):
            if k >> bit & 1:
                value = value + (1 - 2 * lax.rem(lax.div(index, 1 << bit), 2)) * (1 << bit)
        result.append(value)
    return result


def main_kernel(
    sizes,
    hid_hbm, mentor_hbm, w_hbm, mask_hbm,
    wg, hg, div,
    hid, mentor, mask, w, hsend, hrecv, h, tsend, trecv, ssend, srecv, part, theirs_part, gsend, grecv,
    hid_sem, mentor_sem, mask_sem, w_sem,
    hs_sem, hr_sem, ts_sem, tr_sem, ss_sem, sr_sem, ps_sem, pr_sem, gs_sem, gr_sem,
):
    nz, nx, nc = sizes
    n = nz * nx * nc
    own, depth = hid.shape
    rows = own * nz
    vocab = w.shape[0]
    fold = PACK // own
    span = depth // fold
    halves = part.shape[0]
    reach = depth // halves
    unrolled = n <= 16

    z, x, c = lax.axis_index("vocab"), lax.axis_index("rows"), lax.axis_index("teach")
    me = (z * nx + x) * nc + c

    inputs = [
        pltpu.make_async_copy(hid_hbm, hid, hid_sem),
        pltpu.make_async_copy(mentor_hbm, mentor, mentor_sem),
        pltpu.make_async_copy(mask_hbm, mask, mask_sem),
        pltpu.make_async_copy(w_hbm, w, w_sem),
    ]
    for copy in inputs:
        copy.start()

    def others(step):
        if unrolled:
            zs, xs, cs = partners(z, nz), partners(x, nx), partners(c, nc)
            for i in reversed(range(1, n)):
                zz, xx, cc = zs[i // (nx * nc)], xs[i // nc % nx], cs[i % nc]
                step((zz * nx + xx) * nc + cc, {"vocab": zz, "rows": xx, "teach": cc})
            return

        def run(offset, carry):
            d = lax.rem(me + offset, n)
            step(d, {
                "vocab": lax.div(d, nx * nc), "rows": lax.rem(lax.div(d, nc), nx), "teach": lax.rem(d, nc),
            })
            return carry

        lax.fori_loop(1, n, run, 0)

    def same_core(step):
        if unrolled:
            zs, xs = partners(z, nz), partners(x, nx)
            for i in reversed(range(1, nz * nx)):
                zz, xx = zs[i // nx], xs[i % nx]
                step(zz * nx + xx, {"vocab": zz, "rows": xx})
            return

        def run(offset, carry):
            d = lax.rem(z * nx + x + offset, nz * nx)
            step(d, {"vocab": lax.div(d, nx), "rows": lax.rem(d, nx)})
            return carry

        lax.fori_loop(1, nz * nx, run, 0)

    barrier = pltpu.get_barrier_semaphore()

    def greet(at):
        pl.semaphore_signal(barrier, inc=1, device_id=at, device_id_type=pl.DeviceIdType.MESH)

    def greet_line(offset, carry):
        greet({"vocab": lax.rem(z + offset, nz)})
        return carry

    lax.fori_loop(1, nz, greet_line, 0, unroll=nz <= 4)
    for i in range(1, nx * nc):
        greet({"rows": lax.rem(x + i // nc, nx), "teach": lax.rem(c + i % nc, nc)})

    inputs[0].wait()
    hidden = hid[...].astype(jnp.float32)
    packed = jnp.concatenate([hidden[:, k * span:(k + 1) * span] for k in range(fold)], axis=0).astype(jnp.bfloat16)
    hsend[...] = packed
    hrecv[z] = packed
    inputs[1].wait()
    low = mentor[:, :vocab]
    high = mentor[:, vocab:2 * vocab]
    first = c == 0
    mine = jnp.where(first, low, high)
    tsend[:, :vocab] = jnp.where(first, high, low)
    part[...] = jnp.zeros_like(part)
    inputs[2].wait()
    keep = row_to_column(mask[...].astype(jnp.float32), 0, rows)

    pl.semaphore_wait(barrier, nz - 1 + nx * nc - 1)

    def send_hidden(offset, carry):
        pltpu.make_async_remote_copy(
            src_ref=hsend, dst_ref=hrecv.at[z], send_sem=hs_sem, recv_sem=hr_sem,
            device_id={"vocab": lax.rem(z + offset, nz)}, device_id_type=pl.DeviceIdType.MESH,
        ).start()
        return carry

    teacher_copy = pltpu.make_async_remote_copy(
        src_ref=tsend, dst_ref=trecv, send_sem=ts_sem, recv_sem=tr_sem,
        device_id={"teach": 1 - c}, device_id_type=pl.DeviceIdType.MESH,
    )
    teacher_copy.start()
    lax.fori_loop(1, nz, send_hidden, 0, unroll=nz <= 4)

    teacher_copy.wait_recv()
    theirs = trecv[:, :vocab]
    scaled = jnp.concatenate(
        [jnp.where(first, mine, theirs), jnp.where(first, theirs, mine)], axis=0
    ) * (1.0 / smoothing_divisor)
    max_t = jnp.max(scaled, axis=1, keepdims=True)
    weight_t = jnp.exp(scaled - max_t)
    sum_t = jnp.sum(weight_t, axis=1, keepdims=True)

    inputs[3].wait()
    pltpu.make_async_copy(hrecv.at[pl.ds(0, nz - 1)], hrecv.at[pl.ds(0, nz - 1)], hr_sem).wait()
    arrived = [hrecv[k].astype(jnp.float32) for k in range(nz)]
    for k in range(fold):
        h[:, k * span:(k + 1) * span] = jnp.concatenate(
            [a[k * own:(k + 1) * own] for a in arrived], axis=0
        ).astype(jnp.bfloat16)

    student = dot(h[...], w[...], (1, 1)) * (1.0 / smoothing_divisor)
    max_s = jnp.max(student, axis=1, keepdims=True)
    sum_s = jnp.sum(jnp.exp(student - max_s), axis=1, keepdims=True)
    cross = jnp.sum(weight_t * (scaled - student), axis=1, keepdims=True)

    width = ssend.shape[1]
    line = column_to_row([max_s, max_t, sum_s, sum_t, cross], width)
    ssend[...] = line
    srecv[me] = line
    others(
        lambda d, at: pltpu.make_async_remote_copy(
            src_ref=ssend, dst_ref=srecv.at[me], send_sem=ss_sem, recv_sem=sr_sem,
            device_id=at, device_id_type=pl.DeviceIdType.MESH,
        ).start()
    )
    pltpu.make_async_copy(srecv.at[pl.ds(0, n - 1)], srecv.at[pl.ds(0, n - 1)], sr_sem).wait()
    stats = srecv[:, 0, :]
    top = jnp.max(stats, axis=0, keepdims=True)
    scale = jnp.exp(stats - top)
    lane = lax.broadcasted_iota(jnp.int32, stats.shape, 1)
    scale = jnp.where(lane < 4 * rows, pltpu.roll(scale, 2 * rows, 1), pltpu.roll(scale, 3 * rows, 1))
    sums = jnp.sum(stats * scale, axis=0, keepdims=True)
    all_max_s, all_max_t = row_to_column(top, 0, rows), row_to_column(top, 1, rows)
    all_sum_s, all_sum_t, all_cross = (row_to_column(sums, k, rows) for k in (2, 3, 4))
    lse_s = all_max_s + jnp.log(all_sum_s)
    lse_t = all_max_t + jnp.log(all_sum_t)

    grad = (
        keep * (objective_scale * smoothing_divisor) * (jnp.exp(student - lse_s) - jnp.exp(scaled - lse_t))
    ).astype(jnp.bfloat16)

    chips = nz * nx
    place = z * nx + x
    swaps = []
    for s in range(halves):
        term = dot(grad, w[:, s * reach:(s + 1) * reach], (1, 0))
        for k in range(reach // LANES):
            part[s, pl.ds(k, rows, stride=PACK), :] = term[:, k * LANES:(k + 1) * LANES]
        swaps.append(pltpu.make_async_remote_copy(
            src_ref=part.at[s].reshape(chips, nc, PACK, LANES).at[:, 1 - c], dst_ref=theirs_part.at[s],
            send_sem=ps_sem.at[s], recv_sem=pr_sem.at[s],
            device_id={"teach": 1 - c}, device_id_type=pl.DeviceIdType.MESH,
        ))
        swaps[-1].start()
    for s in range(halves):
        swaps[s].wait_recv()
        both = part[s].reshape(chips, nc, PACK, LANES)
        own_part = jnp.where(first, both[:, 0], both[:, 1])
        gsend[s] = (own_part + theirs_part[s]).astype(jnp.bfloat16)
        same_core(
            lambda d, at: pltpu.make_async_remote_copy(
                src_ref=gsend.at[s, d], dst_ref=grecv.at[s, place],
                send_sem=gs_sem.at[s], recv_sem=gr_sem.at[s],
                device_id=at, device_id_type=pl.DeviceIdType.MESH,
            ).start()
        )
        grecv[s, place] = gsend[s, place]

    div[...] = column_to_row([keep * (all_cross / all_sum_t - lse_t + lse_s)], rows)
    step = depth // 7 if depth % (7 * LANES) == 0 else LANES
    for k in range(0, depth, step):
        wg[:, k:k + step] = dot(grad, h[:, k:k + step], (0, 0)).astype(jnp.bfloat16)

    for s in range(halves):
        rest = grecv.at[s, pl.ds(0, chips - 1)]
        pltpu.make_async_copy(rest, rest, gr_sem.at[s]).wait()
        total = jnp.sum(grecv[s].astype(jnp.float32), axis=0)
        for k in range(reach // LANES):
            at = s * reach + k * LANES
            hg[:, at:at + LANES] = total[k:k + 1].astype(jnp.bfloat16)

    pltpu.make_async_copy(hrecv.at[pl.ds(0, nz - 1)], hrecv.at[pl.ds(0, nz - 1)], hs_sem).wait()
    teacher_copy.wait_send()
    for swap in swaps:
        swap.wait_send()
    pltpu.make_async_copy(srecv.at[pl.ds(0, n - 1)], srecv.at[pl.ds(0, n - 1)], ss_sem).wait()
    for s in range(halves):
        rest = grecv.at[s, pl.ds(0, chips - 1)]
        pltpu.make_async_copy(rest, rest, gs_sem.at[s]).wait()


def write_kernel(wg, hg, div, wg_out, hg_out, div_out, wg_sem, hg_sem, div_sem):
    vocab = wg.shape[0]
    slab = -(-vocab // (wg_sem.shape[0] * PACK)) * PACK
    copies = [pltpu.make_async_copy(hg, hg_out, hg_sem), pltpu.make_async_copy(div, div_out, div_sem)]
    for k, first in enumerate(range(0, vocab, slab)):
        at = pl.ds(first, min(slab, vocab - first))
        copies.append(pltpu.make_async_copy(wg.at[at], wg_out.at[at], wg_sem.at[k]))
    for copy in copies:
        copy.start()
    for copy in copies:
        copy.wait()


def body(sizes, hidden_rows, mentor_unnormalized, head_weight, row_mask):
    nz, nx, nc = sizes
    n = nz * nx * nc
    own, depth = hidden_rows.shape
    vocab = head_weight.shape[0]
    rows = own * nz
    half = mentor_unnormalized.shape[0]
    assert rows == n and nc == 2 and PACK % own == 0
    fold = PACK // own
    halves = 2
    assert depth % (halves * LANES) == 0 and depth // (halves * LANES) <= PACK
    wide = -(-vocab // LANES) * LANES
    width = -(-5 * rows // LANES) * LANES
    vmem = pl.BlockSpec(memory_space=pltpu.VMEM)
    hbm = pl.BlockSpec(memory_space=pltpu.HBM)
    dma = pltpu.SemaphoreType.DMA
    results = (
        jax.ShapeDtypeStruct((vocab, depth), jnp.bfloat16),
        jax.ShapeDtypeStruct((1, depth), jnp.bfloat16),
        jax.ShapeDtypeStruct((1, rows), jnp.float32),
    )
    made = pl.pallas_call(
        functools.partial(main_kernel, sizes),
        out_shape=results,
        in_specs=[hbm, hbm, hbm, hbm],
        out_specs=(vmem, vmem, vmem),
        scratch_shapes=[
            pltpu.VMEM((own, depth), jnp.bfloat16),
            pltpu.VMEM(mentor_unnormalized.shape, jnp.float32),
            pltpu.VMEM((1, rows), jnp.int32),
            pltpu.VMEM((vocab, depth), jnp.bfloat16),
            pltpu.VMEM((PACK, depth // fold), jnp.bfloat16),
            pltpu.VMEM((nz, PACK, depth // fold), jnp.bfloat16),
            pltpu.VMEM((rows, depth), jnp.bfloat16),
            pltpu.VMEM((half, wide), jnp.float32),
            pltpu.VMEM((half, wide), jnp.float32),
            pltpu.VMEM((1, width), jnp.float32),
            pltpu.VMEM((n, 1, width), jnp.float32),
            pltpu.VMEM((halves, rows * PACK, LANES), jnp.float32),
            pltpu.VMEM((halves, rows // nc, PACK, LANES), jnp.float32),
            pltpu.VMEM((halves, rows // nc, PACK, LANES), jnp.bfloat16),
            pltpu.VMEM((halves, rows // nc, PACK, LANES), jnp.bfloat16),
        ] + [dma] * 10 + [dma((halves,))] * 4,
        compiler_params=pltpu.CompilerParams(
            collective_id=0, has_side_effects=True, vmem_limit_bytes=44 * 2**20
        ),
    )(*(
        pltpu.with_memory_space_constraint(a, pltpu.HBM)
        for a in (hidden_rows, mentor_unnormalized, head_weight, row_mask.reshape(1, rows))
    ))
    wg, hg, div = pl.pallas_call(
        write_kernel,
        out_shape=results,
        in_specs=[vmem, vmem, vmem],
        out_specs=(hbm, hbm, hbm),
        scratch_shapes=[dma((4,)), dma, dma],
        compiler_params=pltpu.CompilerParams(vmem_limit_bytes=4 * 2**20),
    )(*(pltpu.with_memory_space_constraint(a, pltpu.VMEM) for a in made))
    return div.reshape(rows), hg, wg


def solution(mesh):
    sizes = (mesh.shape["vocab"], mesh.shape["rows"], mesh.shape["teach"])
    return jax.shard_map(
        functools.partial(body, sizes),
        mesh=mesh,
        in_specs=(
            P(("groups", "vocab"), None),
            P(("groups", "teach"), ("vocab", "rows")),
            P(("vocab", "rows", "teach"), None),
            P("groups"),
        ),
        out_specs=(
            P("groups"),
            P(("groups", "vocab", "rows", "teach"), None),
            P(("groups", "vocab", "rows", "teach"), None),
        ),
        check_vma=False,
    )
```

```python
import functools

import jax
import jax.numpy as jnp
from jax import lax
from jax.experimental import pallas as pl
from jax.experimental.pallas import tpu as pltpu
from jax.sharding import PartitionSpec as P

smoothing_divisor = 2.0
objective_scale = 256.0

LANES = 128
PACK = 16


def dot(a, b, contract):
    return lax.dot_general(a, b, ((contract[:1], contract[1:]), ((), ())), preferred_element_type=jnp.float32)


def column_to_row(columns, width):
    rows = columns[0].shape[0]
    lane = lax.broadcasted_iota(jnp.int32, (rows, width), 1)
    row = lax.broadcasted_iota(jnp.int32, (rows, width), 0)
    total = jnp.zeros((rows, width), jnp.float32)
    for place, column in enumerate(columns):
        total = jnp.where(lane == row + place * rows, column, total)
    return jnp.sum(total, axis=0, keepdims=True)


def row_to_column(line, place, rows):
    width = line.shape[1]
    lane = lax.broadcasted_iota(jnp.int32, (rows, width), 1)
    row = lax.broadcasted_iota(jnp.int32, (rows, width), 0)
    return jnp.sum(jnp.where(lane == row + place * rows, line, 0.0), axis=1, keepdims=True)


def partners(index, size):
    if size & (size - 1):
        return [index] + [lax.rem(index + k, size) for k in range(1, size)]
    result = []
    for k in range(size):
        value = index
        for bit in range(size.bit_length() - 1):
            if k >> bit & 1:
                value = value + (1 - 2 * lax.rem(lax.div(index, 1 << bit), 2)) * (1 << bit)
        result.append(value)
    return result


def main_kernel(
    sizes,
    hid_hbm, mentor_hbm, w_hbm, mask_hbm,
    wg, hg, div,
    hid, mentor, mask, w, hsend, direct, relayed, h, tsend, trecv, ssend, srecv, part, theirs_part, gsend, grecv,
    hid_sem, mentor_sem, mask_sem, w_sem,
    hs_sem, rs_sem, rr_sem, ts_sem, tr_sem, ss_sem, sr_sem, hr_sem, ps_sem, pr_sem, gs_sem, gr_sem,
):
    nz, nx, nc = sizes
    n = nz * nx * nc
    own, depth = hid.shape
    rows = own * nz
    vocab = w.shape[0]
    fold = PACK // own
    span = depth // fold
    halves = part.shape[0]
    reach = depth // halves
    unrolled = n <= 16

    z, x, c = lax.axis_index("vocab"), lax.axis_index("rows"), lax.axis_index("teach")
    me = (z * nx + x) * nc + c

    inputs = [
        pltpu.make_async_copy(hid_hbm, hid, hid_sem),
        pltpu.make_async_copy(mentor_hbm, mentor, mentor_sem),
        pltpu.make_async_copy(mask_hbm, mask, mask_sem),
        pltpu.make_async_copy(w_hbm, w, w_sem),
    ]
    for copy in inputs:
        copy.start()

    def others(step):
        if unrolled:
            zs, xs, cs = partners(z, nz), partners(x, nx), partners(c, nc)
            for i in reversed(range(1, n)):
                zz, xx, cc = zs[i // (nx * nc)], xs[i // nc % nx], cs[i % nc]
                step((zz * nx + xx) * nc + cc, {"vocab": zz, "rows": xx, "teach": cc})
            return

        def run(offset, carry):
            d = lax.rem(me + offset, n)
            step(d, {
                "vocab": lax.div(d, nx * nc), "rows": lax.rem(lax.div(d, nc), nx), "teach": lax.rem(d, nc),
            })
            return carry

        lax.fori_loop(1, n, run, 0)

    def same_core(step):
        if unrolled:
            zs, xs = partners(z, nz), partners(x, nx)
            for i in reversed(range(1, nz * nx)):
                zz, xx = zs[i // nx], xs[i % nx]
                step(zz * nx + xx, {"vocab": zz, "rows": xx})
            return

        def run(offset, carry):
            d = lax.rem(z * nx + x + offset, nz * nx)
            step(d, {"vocab": lax.div(d, nx), "rows": lax.rem(d, nx)})
            return carry

        lax.fori_loop(1, nz * nx, run, 0)

    barrier = pltpu.get_barrier_semaphore()

    def greet(at):
        pl.semaphore_signal(barrier, inc=1, device_id=at, device_id_type=pl.DeviceIdType.MESH)

    def greet_line(offset, carry):
        greet({"vocab": lax.rem(z + offset, nz)})
        return carry

    lax.fori_loop(1, nz, greet_line, 0, unroll=nz <= 4)
    for i in range(1, nx * nc):
        greet({"rows": lax.rem(x + i // nc, nx), "teach": lax.rem(c + i % nc, nc)})

    first = c == 0
    piece = direct.shape[2]
    rest_of = span - piece
    inputs[0].wait()
    hidden = hid[...].astype(jnp.float32)
    packed = jnp.concatenate([hidden[:, k * span:(k + 1) * span] for k in range(fold)], axis=0).astype(jnp.bfloat16)
    low, high = packed[:, :piece], packed[:, rest_of:]
    hsend[...] = jnp.where(first, low, high)
    direct[z] = jnp.where(first, low, high)
    relayed[z] = jnp.where(first, high, low)

    pl.semaphore_wait(barrier, nz - 1 + nx * nc - 1)

    def send_hidden(to):
        pltpu.make_async_remote_copy(
            src_ref=hsend, dst_ref=direct.at[z], send_sem=hs_sem, recv_sem=hr_sem.at[z],
            device_id={"vocab": to}, device_id_type=pl.DeviceIdType.MESH,
        ).start()

    def relay(source):
        pltpu.make_async_copy(hsend, direct.at[source], hr_sem.at[source]).wait()
        pltpu.make_async_remote_copy(
            src_ref=direct.at[source], dst_ref=relayed.at[source], send_sem=rs_sem, recv_sem=rr_sem,
            device_id={"teach": 1 - c}, device_id_type=pl.DeviceIdType.MESH,
        ).start()

    def line(step, far_first):
        if unrolled:
            peers = partners(z, nz)[1:]
            for zz in reversed(peers) if far_first else peers:
                step(zz)
            return

        def run(offset, carry):
            step(lax.rem(z + offset, nz))
            return carry

        lax.fori_loop(1, nz, run, 0)

    line(send_hidden, True)

    inputs[1].wait()
    low = mentor[:, :vocab]
    high = mentor[:, vocab:2 * vocab]
    mine = jnp.where(first, low, high)
    tsend[:, :vocab] = jnp.where(first, high, low)
    teacher_copy = pltpu.make_async_remote_copy(
        src_ref=tsend, dst_ref=trecv, send_sem=ts_sem, recv_sem=tr_sem,
        device_id={"teach": 1 - c}, device_id_type=pl.DeviceIdType.MESH,
    )
    teacher_copy.start()
    part[...] = jnp.zeros_like(part)
    inputs[2].wait()
    keep = row_to_column(mask[...].astype(jnp.float32), 0, rows)

    line(relay, False)

    teacher_copy.wait_recv()
    theirs = trecv[:, :vocab]
    scaled = jnp.concatenate(
        [jnp.where(first, mine, theirs), jnp.where(first, theirs, mine)], axis=0
    ) * (1.0 / smoothing_divisor)
    max_t = jnp.max(scaled, axis=1, keepdims=True)
    weight_t = jnp.exp(scaled - max_t)
    sum_t = jnp.sum(weight_t, axis=1, keepdims=True)

    inputs[3].wait()
    peers = relayed.at[pl.ds(0, nz - 1)]
    pltpu.make_async_copy(peers, peers, rr_sem).wait()
    arrived = []
    for k in range(nz):
        low = jnp.where(first, direct[k], relayed[k])
        high = jnp.where(first, relayed[k], direct[k])
        arrived.append(jnp.concatenate([low, high[:, piece - rest_of:]], axis=1).astype(jnp.float32))
    for k in range(fold):
        h[:, k * span:(k + 1) * span] = jnp.concatenate(
            [a[k * own:(k + 1) * own] for a in arrived], axis=0
        ).astype(jnp.bfloat16)

    student = dot(h[...], w[...], (1, 1)) * (1.0 / smoothing_divisor)
    max_s = jnp.max(student, axis=1, keepdims=True)
    sum_s = jnp.sum(jnp.exp(student - max_s), axis=1, keepdims=True)
    cross = jnp.sum(weight_t * (scaled - student), axis=1, keepdims=True)

    width = ssend.shape[1]
    line = column_to_row([max_s, max_t, sum_s, sum_t, cross], width)
    ssend[...] = line
    srecv[me] = line
    others(
        lambda d, at: pltpu.make_async_remote_copy(
            src_ref=ssend, dst_ref=srecv.at[me], send_sem=ss_sem, recv_sem=sr_sem,
            device_id=at, device_id_type=pl.DeviceIdType.MESH,
        ).start()
    )
    pltpu.make_async_copy(srecv.at[pl.ds(0, n - 1)], srecv.at[pl.ds(0, n - 1)], sr_sem).wait()
    stats = srecv[:, 0, :]
    top = jnp.max(stats, axis=0, keepdims=True)
    scale = jnp.exp(stats - top)
    lane = lax.broadcasted_iota(jnp.int32, stats.shape, 1)
    scale = jnp.where(lane < 4 * rows, pltpu.roll(scale, 2 * rows, 1), pltpu.roll(scale, 3 * rows, 1))
    sums = jnp.sum(stats * scale, axis=0, keepdims=True)
    all_max_s, all_max_t = row_to_column(top, 0, rows), row_to_column(top, 1, rows)
    all_sum_s, all_sum_t, all_cross = (row_to_column(sums, k, rows) for k in (2, 3, 4))
    lse_s = all_max_s + jnp.log(all_sum_s)
    lse_t = all_max_t + jnp.log(all_sum_t)

    grad = (
        keep * (objective_scale * smoothing_divisor) * (jnp.exp(student - lse_s) - jnp.exp(scaled - lse_t))
    ).astype(jnp.bfloat16)

    chips = nz * nx
    place = z * nx + x
    swaps = []
    for s in range(halves):
        term = dot(grad, w[:, s * reach:(s + 1) * reach], (1, 0))
        for k in range(reach // LANES):
            part[s, pl.ds(k, rows, stride=PACK), :] = term[:, k * LANES:(k + 1) * LANES]
        swaps.append(pltpu.make_async_remote_copy(
            src_ref=part.at[s].reshape(chips, nc, PACK, LANES).at[:, 1 - c], dst_ref=theirs_part.at[s],
            send_sem=ps_sem.at[s], recv_sem=pr_sem.at[s],
            device_id={"teach": 1 - c}, device_id_type=pl.DeviceIdType.MESH,
        ))
        swaps[-1].start()
    for s in range(halves):
        swaps[s].wait_recv()
        both = part[s].reshape(chips, nc, PACK, LANES)
        own_part = jnp.where(first, both[:, 0], both[:, 1])
        gsend[s] = (own_part + theirs_part[s]).astype(jnp.bfloat16)
        same_core(
            lambda d, at: pltpu.make_async_remote_copy(
                src_ref=gsend.at[s, d], dst_ref=grecv.at[s, place],
                send_sem=gs_sem.at[s], recv_sem=gr_sem.at[s],
                device_id=at, device_id_type=pl.DeviceIdType.MESH,
            ).start()
        )
        grecv[s, place] = gsend[s, place]

    div[...] = column_to_row([keep * (all_cross / all_sum_t - lse_t + lse_s)], rows)
    step = depth // 7 if depth % (7 * LANES) == 0 else LANES
    for k in range(0, depth, step):
        wg[:, k:k + step] = dot(grad, h[:, k:k + step], (0, 0)).astype(jnp.bfloat16)

    for s in range(halves):
        rest = grecv.at[s, pl.ds(0, chips - 1)]
        pltpu.make_async_copy(rest, rest, gr_sem.at[s]).wait()
        total = jnp.sum(grecv[s].astype(jnp.float32), axis=0)
        for k in range(reach // LANES):
            at = s * reach + k * LANES
            hg[:, at:at + LANES] = total[k:k + 1].astype(jnp.bfloat16)

    pltpu.make_async_copy(peers, peers, hs_sem).wait()
    pltpu.make_async_copy(peers, peers, rs_sem).wait()
    teacher_copy.wait_send()
    for swap in swaps:
        swap.wait_send()
    pltpu.make_async_copy(srecv.at[pl.ds(0, n - 1)], srecv.at[pl.ds(0, n - 1)], ss_sem).wait()
    for s in range(halves):
        rest = grecv.at[s, pl.ds(0, chips - 1)]
        pltpu.make_async_copy(rest, rest, gs_sem.at[s]).wait()


def write_kernel(wg, hg, div, wg_out, hg_out, div_out, wg_sem, hg_sem, div_sem):
    vocab = wg.shape[0]
    slab = -(-vocab // (wg_sem.shape[0] * PACK)) * PACK
    copies = [pltpu.make_async_copy(hg, hg_out, hg_sem), pltpu.make_async_copy(div, div_out, div_sem)]
    for k, first in enumerate(range(0, vocab, slab)):
        at = pl.ds(first, min(slab, vocab - first))
        copies.append(pltpu.make_async_copy(wg.at[at], wg_out.at[at], wg_sem.at[k]))
    for copy in copies:
        copy.start()
    for copy in copies:
        copy.wait()


def body(sizes, hidden_rows, mentor_unnormalized, head_weight, row_mask):
    nz, nx, nc = sizes
    n = nz * nx * nc
    own, depth = hidden_rows.shape
    vocab = head_weight.shape[0]
    rows = own * nz
    half = mentor_unnormalized.shape[0]
    assert rows == n and nc == 2 and PACK % own == 0
    fold = PACK // own
    assert depth % (fold * LANES) == 0
    piece = -(-depth // (fold * nc * LANES)) * LANES
    halves = 2
    assert depth % (halves * LANES) == 0 and depth // (halves * LANES) <= PACK
    wide = -(-vocab // LANES) * LANES
    width = -(-5 * rows // LANES) * LANES
    vmem = pl.BlockSpec(memory_space=pltpu.VMEM)
    hbm = pl.BlockSpec(memory_space=pltpu.HBM)
    dma = pltpu.SemaphoreType.DMA
    results = (
        jax.ShapeDtypeStruct((vocab, depth), jnp.bfloat16),
        jax.ShapeDtypeStruct((1, depth), jnp.bfloat16),
        jax.ShapeDtypeStruct((1, rows), jnp.float32),
    )
    made = pl.pallas_call(
        functools.partial(main_kernel, sizes),
        out_shape=results,
        in_specs=[hbm, hbm, hbm, hbm],
        out_specs=(vmem, vmem, vmem),
        scratch_shapes=[
            pltpu.VMEM((own, depth), jnp.bfloat16),
            pltpu.VMEM(mentor_unnormalized.shape, jnp.float32),
            pltpu.VMEM((1, rows), jnp.int32),
            pltpu.VMEM((vocab, depth), jnp.bfloat16),
            pltpu.VMEM((PACK, piece), jnp.bfloat16),
            pltpu.VMEM((nz, PACK, piece), jnp.bfloat16),
            pltpu.VMEM((nz, PACK, piece), jnp.bfloat16),
            pltpu.VMEM((rows, depth), jnp.bfloat16),
            pltpu.VMEM((half, wide), jnp.float32),
            pltpu.VMEM((half, wide), jnp.float32),
            pltpu.VMEM((1, width), jnp.float32),
            pltpu.VMEM((n, 1, width), jnp.float32),
            pltpu.VMEM((halves, rows * PACK, LANES), jnp.float32),
            pltpu.VMEM((halves, rows // nc, PACK, LANES), jnp.float32),
            pltpu.VMEM((halves, rows // nc, PACK, LANES), jnp.bfloat16),
            pltpu.VMEM((halves, rows // nc, PACK, LANES), jnp.bfloat16),
        ] + [dma] * 11 + [dma((nz,))] + [dma((halves,))] * 4,
        compiler_params=pltpu.CompilerParams(
            collective_id=0, has_side_effects=True, vmem_limit_bytes=44 * 2**20
        ),
    )(*(
        pltpu.with_memory_space_constraint(a, pltpu.HBM)
        for a in (hidden_rows, mentor_unnormalized, head_weight, row_mask.reshape(1, rows))
    ))
    wg, hg, div = pl.pallas_call(
        write_kernel,
        out_shape=results,
        in_specs=[vmem, vmem, vmem],
        out_specs=(hbm, hbm, hbm),
        scratch_shapes=[dma((4,)), dma, dma],
        compiler_params=pltpu.CompilerParams(vmem_limit_bytes=4 * 2**20),
    )(*(pltpu.with_memory_space_constraint(a, pltpu.VMEM) for a in made))
    return div.reshape(rows), hg, wg


def solution(mesh):
    sizes = (mesh.shape["vocab"], mesh.shape["rows"], mesh.shape["teach"])
    return jax.shard_map(
        functools.partial(body, sizes),
        mesh=mesh,
        in_specs=(
            P(("groups", "vocab"), None),
            P(("groups", "teach"), ("vocab", "rows")),
            P(("vocab", "rows", "teach"), None),
            P("groups"),
        ),
        out_specs=(
            P("groups"),
            P(("groups", "vocab", "rows", "teach"), None),
            P(("groups", "vocab", "rows", "teach"), None),
        ),
        check_vma=False,
    )
```

```python
import functools

import jax
import jax.numpy as jnp
from jax import lax
from jax.experimental import pallas as pl
from jax.experimental.pallas import tpu as pltpu
from jax.sharding import PartitionSpec as P

smoothing_divisor = 2.0
objective_scale = 256.0

LANES = 128
PACK = 16


def dot(a, b, contract):
    return lax.dot_general(a, b, ((contract[:1], contract[1:]), ((), ())), preferred_element_type=jnp.float32)


def column_to_row(columns, width):
    rows = columns[0].shape[0]
    lane = lax.broadcasted_iota(jnp.int32, (rows, width), 1)
    row = lax.broadcasted_iota(jnp.int32, (rows, width), 0)
    total = jnp.zeros((rows, width), jnp.float32)
    for place, column in enumerate(columns):
        total = jnp.where(lane == row + place * rows, column, total)
    return jnp.sum(total, axis=0, keepdims=True)


def row_to_column(line, place, rows):
    width = line.shape[1]
    lane = lax.broadcasted_iota(jnp.int32, (rows, width), 1)
    row = lax.broadcasted_iota(jnp.int32, (rows, width), 0)
    return jnp.sum(jnp.where(lane == row + place * rows, line, 0.0), axis=1, keepdims=True)


def partners(index, size):
    if size & (size - 1):
        return [index] + [lax.rem(index + k, size) for k in range(1, size)]
    result = []
    for k in range(size):
        value = index
        for bit in range(size.bit_length() - 1):
            if k >> bit & 1:
                value = value + (1 - 2 * lax.rem(lax.div(index, 1 << bit), 2)) * (1 << bit)
        result.append(value)
    return result


def main_kernel(
    sizes,
    hid_hbm, mentor_hbm, w_hbm, mask_hbm,
    wg, hg, div,
    hid, mentor, mask, w, hsend, direct, relayed, h, tsend, trecv, ssend, srecv, part, theirs_part, gsend, grecv,
    hid_sem, mentor_sem, mask_sem, w_sem,
    hs_sem, rs_sem, rr_sem, ts_sem, tr_sem, ss_sem, sr_sem, hr_sem, ps_sem, pr_sem, gs_sem, gr_sem,
):
    nz, nx, nc = sizes
    n = nz * nx * nc
    own, depth = hid.shape
    rows = own * nz
    vocab = w.shape[0]
    fold = PACK // own
    span = depth // fold
    halves = part.shape[0]
    reach = depth // halves
    unrolled = n <= 16

    z, x, c = lax.axis_index("vocab"), lax.axis_index("rows"), lax.axis_index("teach")
    me = (z * nx + x) * nc + c

    inputs = [
        pltpu.make_async_copy(hid_hbm, hid, hid_sem),
        pltpu.make_async_copy(mentor_hbm, mentor, mentor_sem),
        pltpu.make_async_copy(mask_hbm, mask, mask_sem),
        pltpu.make_async_copy(w_hbm, w, w_sem),
    ]
    for copy in inputs:
        copy.start()

    def others(step):
        if unrolled:
            zs, xs, cs = partners(z, nz), partners(x, nx), partners(c, nc)
            for i in reversed(range(1, n)):
                zz, xx, cc = zs[i // (nx * nc)], xs[i // nc % nx], cs[i % nc]
                step((zz * nx + xx) * nc + cc, {"vocab": zz, "rows": xx, "teach": cc})
            return

        def run(offset, carry):
            d = lax.rem(me + offset, n)
            step(d, {
                "vocab": lax.div(d, nx * nc), "rows": lax.rem(lax.div(d, nc), nx), "teach": lax.rem(d, nc),
            })
            return carry

        lax.fori_loop(1, n, run, 0)

    def same_core(step):
        if unrolled:
            zs, xs = partners(z, nz), partners(x, nx)
            for i in reversed(range(1, nz * nx)):
                zz, xx = zs[i // nx], xs[i % nx]
                step(zz * nx + xx, {"vocab": zz, "rows": xx})
            return

        def run(offset, carry):
            d = lax.rem(z * nx + x + offset, nz * nx)
            step(d, {"vocab": lax.div(d, nx), "rows": lax.rem(d, nx)})
            return carry

        lax.fori_loop(1, nz * nx, run, 0)

    barrier = pltpu.get_barrier_semaphore()

    def greet(at):
        pl.semaphore_signal(barrier, inc=1, device_id=at, device_id_type=pl.DeviceIdType.MESH)

    def greet_line(offset, carry):
        greet({"vocab": lax.rem(z + offset, nz)})
        return carry

    lax.fori_loop(1, nz, greet_line, 0, unroll=nz <= 4)
    for i in range(1, nx * nc):
        greet({"rows": lax.rem(x + i // nc, nx), "teach": lax.rem(c + i % nc, nc)})

    first = c == 0
    piece = direct.shape[2]
    rest_of = span - piece
    inputs[0].wait()
    hidden = hid[...].astype(jnp.float32)
    packed = jnp.concatenate([hidden[:, k * span:(k + 1) * span] for k in range(fold)], axis=0).astype(jnp.bfloat16)
    low, high = packed[:, :piece], packed[:, rest_of:]
    hsend[...] = jnp.where(first, low, high)
    direct[z] = jnp.where(first, low, high)
    relayed[z] = jnp.where(first, high, low)

    pl.semaphore_wait(barrier, nz - 1 + nx * nc - 1)

    def send_hidden(to):
        pltpu.make_async_remote_copy(
            src_ref=hsend, dst_ref=direct.at[z], send_sem=hs_sem, recv_sem=hr_sem.at[z],
            device_id={"vocab": to}, device_id_type=pl.DeviceIdType.MESH,
        ).start()

    def relay(source):
        pltpu.make_async_copy(hsend, direct.at[source], hr_sem.at[source]).wait()
        pltpu.make_async_remote_copy(
            src_ref=direct.at[source], dst_ref=relayed.at[source], send_sem=rs_sem, recv_sem=rr_sem,
            device_id={"teach": 1 - c}, device_id_type=pl.DeviceIdType.MESH,
        ).start()

    def line(step, far_first):
        if unrolled:
            peers = partners(z, nz)[1:]
            for zz in reversed(peers) if far_first else peers:
                step(zz)
            return

        def run(offset, carry):
            step(lax.rem(z + offset, nz))
            return carry

        lax.fori_loop(1, nz, run, 0)

    line(send_hidden, True)

    inputs[1].wait()
    low = mentor[:, :vocab]
    high = mentor[:, vocab:2 * vocab]
    mine = jnp.where(first, low, high)
    tsend[:, :vocab] = jnp.where(first, high, low)
    teacher_copy = pltpu.make_async_remote_copy(
        src_ref=tsend, dst_ref=trecv, send_sem=ts_sem, recv_sem=tr_sem,
        device_id={"teach": 1 - c}, device_id_type=pl.DeviceIdType.MESH,
    )
    teacher_copy.start()
    part[...] = jnp.zeros_like(part)
    inputs[2].wait()
    keep = row_to_column(mask[...].astype(jnp.float32), 0, rows)

    line(relay, False)

    teacher_copy.wait_recv()
    theirs = trecv[:, :vocab]
    scaled = jnp.concatenate(
        [jnp.where(first, mine, theirs), jnp.where(first, theirs, mine)], axis=0
    ) * (1.0 / smoothing_divisor)
    max_t = jnp.max(scaled, axis=1, keepdims=True)
    weight_t = jnp.exp(scaled - max_t)
    sum_t = jnp.sum(weight_t, axis=1, keepdims=True)

    inputs[3].wait()

    def columns_of(held, k, start, width):
        return jnp.concatenate(
            [held[zz, :, pl.ds(start, width)][k * own:(k + 1) * own].astype(jnp.float32) for zz in range(nz)], axis=0
        ).astype(jnp.bfloat16)

    logits = jnp.zeros((rows, vocab), jnp.float32)
    for k in range(fold):
        at = pl.multiple_of(k * span + c * rest_of, LANES)
        logits += dot(columns_of(direct, k, 0, piece), w[:, pl.ds(at, piece)], (1, 1))
    peers = relayed.at[pl.ds(0, nz - 1)]
    pltpu.make_async_copy(peers, peers, rr_sem).wait()
    for k in range(fold):
        start = pl.multiple_of((1 - c) * (piece - rest_of), LANES)
        at = pl.multiple_of(k * span + (1 - c) * piece, LANES)
        logits += dot(columns_of(relayed, k, start, rest_of), w[:, pl.ds(at, rest_of)], (1, 1))

    student = logits * (1.0 / smoothing_divisor)
    max_s = jnp.max(student, axis=1, keepdims=True)
    weight_s = jnp.exp(student - max_s)
    sum_s = jnp.sum(weight_s, axis=1, keepdims=True)
    cross = jnp.sum(weight_t * (scaled - student), axis=1, keepdims=True)

    width = ssend.shape[1]
    line = column_to_row([max_s, max_t, sum_s, sum_t, cross], width)
    ssend[...] = line
    srecv[me] = line
    others(
        lambda d, at: pltpu.make_async_remote_copy(
            src_ref=ssend, dst_ref=srecv.at[me], send_sem=ss_sem, recv_sem=sr_sem,
            device_id=at, device_id_type=pl.DeviceIdType.MESH,
        ).start()
    )
    arrived = []
    for k in range(nz):
        low = jnp.where(first, direct[k], relayed[k])
        high = jnp.where(first, relayed[k], direct[k])
        arrived.append(jnp.concatenate([low, high[:, piece - rest_of:]], axis=1).astype(jnp.float32))
    for k in range(fold):
        h[:, k * span:(k + 1) * span] = jnp.concatenate(
            [a[k * own:(k + 1) * own] for a in arrived], axis=0
        ).astype(jnp.bfloat16)
    pltpu.make_async_copy(srecv.at[pl.ds(0, n - 1)], srecv.at[pl.ds(0, n - 1)], sr_sem).wait()
    stats = srecv[:, 0, :]
    top = jnp.max(stats, axis=0, keepdims=True)
    scale = jnp.exp(stats - top)
    lane = lax.broadcasted_iota(jnp.int32, stats.shape, 1)
    scale = jnp.where(lane < 4 * rows, pltpu.roll(scale, 2 * rows, 1), pltpu.roll(scale, 3 * rows, 1))
    sums = jnp.sum(stats * scale, axis=0, keepdims=True)
    all_max_s, all_max_t = row_to_column(top, 0, rows), row_to_column(top, 1, rows)
    all_sum_s, all_sum_t, all_cross = (row_to_column(sums, k, rows) for k in (2, 3, 4))
    lse_s = all_max_s + jnp.log(all_sum_s)
    lse_t = all_max_t + jnp.log(all_sum_t)

    factor = keep * (objective_scale * smoothing_divisor)
    grad = (
        weight_s * (factor * jnp.exp(max_s - lse_s)) - weight_t * (factor * jnp.exp(max_t - lse_t))
    ).astype(jnp.bfloat16)

    chips = nz * nx
    place = z * nx + x
    swaps = []
    for s in range(halves):
        term = dot(grad, w[:, s * reach:(s + 1) * reach], (1, 0))
        for k in range(reach // LANES):
            part[s, pl.ds(k, rows, stride=PACK), :] = term[:, k * LANES:(k + 1) * LANES]
        swaps.append(pltpu.make_async_remote_copy(
            src_ref=part.at[s].reshape(chips, nc, PACK, LANES).at[:, 1 - c], dst_ref=theirs_part.at[s],
            send_sem=ps_sem.at[s], recv_sem=pr_sem.at[s],
            device_id={"teach": 1 - c}, device_id_type=pl.DeviceIdType.MESH,
        ))
        swaps[-1].start()
    for s in range(halves):
        swaps[s].wait_recv()
        both = part[s].reshape(chips, nc, PACK, LANES)
        own_part = jnp.where(first, both[:, 0], both[:, 1])
        gsend[s] = (own_part + theirs_part[s]).astype(jnp.bfloat16)
        same_core(
            lambda d, at: pltpu.make_async_remote_copy(
                src_ref=gsend.at[s, d], dst_ref=grecv.at[s, place],
                send_sem=gs_sem.at[s], recv_sem=gr_sem.at[s],
                device_id=at, device_id_type=pl.DeviceIdType.MESH,
            ).start()
        )
        grecv[s, place] = gsend[s, place]

    div[...] = column_to_row([keep * (all_cross / all_sum_t - lse_t + lse_s)], rows)
    step = depth // 7 if depth % (7 * LANES) == 0 else LANES
    for k in range(0, depth, step):
        wg[:, k:k + step] = dot(grad, h[:, k:k + step], (0, 0)).astype(jnp.bfloat16)

    for s in range(halves):
        rest = grecv.at[s, pl.ds(0, chips - 1)]
        pltpu.make_async_copy(rest, rest, gr_sem.at[s]).wait()
        total = jnp.sum(grecv[s].astype(jnp.float32), axis=0)
        for k in range(reach // LANES):
            at = s * reach + k * LANES
            hg[:, at:at + LANES] = total[k:k + 1].astype(jnp.bfloat16)

    pltpu.make_async_copy(peers, peers, hs_sem).wait()
    pltpu.make_async_copy(peers, peers, rs_sem).wait()
    teacher_copy.wait_send()
    for swap in swaps:
        swap.wait_send()
    pltpu.make_async_copy(srecv.at[pl.ds(0, n - 1)], srecv.at[pl.ds(0, n - 1)], ss_sem).wait()
    for s in range(halves):
        rest = grecv.at[s, pl.ds(0, chips - 1)]
        pltpu.make_async_copy(rest, rest, gs_sem.at[s]).wait()


def write_kernel(wg, hg, div, wg_out, hg_out, div_out, wg_sem, hg_sem, div_sem):
    vocab = wg.shape[0]
    slab = -(-vocab // (wg_sem.shape[0] * PACK)) * PACK
    copies = [pltpu.make_async_copy(hg, hg_out, hg_sem), pltpu.make_async_copy(div, div_out, div_sem)]
    for k, first in enumerate(range(0, vocab, slab)):
        at = pl.ds(first, min(slab, vocab - first))
        copies.append(pltpu.make_async_copy(wg.at[at], wg_out.at[at], wg_sem.at[k]))
    for copy in copies:
        copy.start()
    for copy in copies:
        copy.wait()


def body(sizes, hidden_rows, mentor_unnormalized, head_weight, row_mask):
    nz, nx, nc = sizes
    n = nz * nx * nc
    own, depth = hidden_rows.shape
    vocab = head_weight.shape[0]
    rows = own * nz
    half = mentor_unnormalized.shape[0]
    assert rows == n and nc == 2 and PACK % own == 0
    fold = PACK // own
    assert depth % (fold * LANES) == 0
    piece = -(-depth // (fold * nc * LANES)) * LANES
    halves = 2
    assert depth % (halves * LANES) == 0 and depth // (halves * LANES) <= PACK
    wide = -(-vocab // LANES) * LANES
    width = -(-5 * rows // LANES) * LANES
    vmem = pl.BlockSpec(memory_space=pltpu.VMEM)
    hbm = pl.BlockSpec(memory_space=pltpu.HBM)
    dma = pltpu.SemaphoreType.DMA
    results = (
        jax.ShapeDtypeStruct((vocab, depth), jnp.bfloat16),
        jax.ShapeDtypeStruct((1, depth), jnp.bfloat16),
        jax.ShapeDtypeStruct((1, rows), jnp.float32),
    )
    made = pl.pallas_call(
        functools.partial(main_kernel, sizes),
        out_shape=results,
        in_specs=[hbm, hbm, hbm, hbm],
        out_specs=(vmem, vmem, vmem),
        scratch_shapes=[
            pltpu.VMEM((own, depth), jnp.bfloat16),
            pltpu.VMEM(mentor_unnormalized.shape, jnp.float32),
            pltpu.VMEM((1, rows), jnp.int32),
            pltpu.VMEM((vocab, depth), jnp.bfloat16),
            pltpu.VMEM((PACK, piece), jnp.bfloat16),
            pltpu.VMEM((nz, PACK, piece), jnp.bfloat16),
            pltpu.VMEM((nz, PACK, piece), jnp.bfloat16),
            pltpu.VMEM((rows, depth), jnp.bfloat16),
            pltpu.VMEM((half, wide), jnp.float32),
            pltpu.VMEM((half, wide), jnp.float32),
            pltpu.VMEM((1, width), jnp.float32),
            pltpu.VMEM((n, 1, width), jnp.float32),
            pltpu.VMEM((halves, rows * PACK, LANES), jnp.float32),
            pltpu.VMEM((halves, rows // nc, PACK, LANES), jnp.float32),
            pltpu.VMEM((halves, rows // nc, PACK, LANES), jnp.bfloat16),
            pltpu.VMEM((halves, rows // nc, PACK, LANES), jnp.bfloat16),
        ] + [dma] * 11 + [dma((nz,))] + [dma((halves,))] * 4,
        compiler_params=pltpu.CompilerParams(
            collective_id=0, has_side_effects=True, vmem_limit_bytes=44 * 2**20
        ),
    )(*(
        pltpu.with_memory_space_constraint(a, pltpu.HBM)
        for a in (hidden_rows, mentor_unnormalized, head_weight, row_mask.reshape(1, rows))
    ))
    wg, hg, div = pl.pallas_call(
        write_kernel,
        out_shape=results,
        in_specs=[vmem, vmem, vmem],
        out_specs=(hbm, hbm, hbm),
        scratch_shapes=[dma((4,)), dma, dma],
        compiler_params=pltpu.CompilerParams(vmem_limit_bytes=4 * 2**20),
    )(*(pltpu.with_memory_space_constraint(a, pltpu.VMEM) for a in made))
    return div.reshape(rows), hg, wg


def solution(mesh):
    sizes = (mesh.shape["vocab"], mesh.shape["rows"], mesh.shape["teach"])
    return jax.shard_map(
        functools.partial(body, sizes),
        mesh=mesh,
        in_specs=(
            P(("groups", "vocab"), None),
            P(("groups", "teach"), ("vocab", "rows")),
            P(("vocab", "rows", "teach"), None),
            P("groups"),
        ),
        out_specs=(
            P("groups"),
            P(("groups", "vocab", "rows", "teach"), None),
            P(("groups", "vocab", "rows", "teach"), None),
        ),
        check_vma=False,
    )
```

```python
import functools

import jax
import jax.numpy as jnp
from jax import lax
from jax.experimental import pallas as pl
from jax.experimental.pallas import tpu as pltpu
from jax.sharding import PartitionSpec as P

smoothing_divisor = 2.0
objective_scale = 256.0

LANES = 128
PACK = 16


def dot(a, b, contract):
    return lax.dot_general(a, b, ((contract[:1], contract[1:]), ((), ())), preferred_element_type=jnp.float32)


def column_to_row(columns, width):
    rows = columns[0].shape[0]
    lane = lax.broadcasted_iota(jnp.int32, (rows, width), 1)
    row = lax.broadcasted_iota(jnp.int32, (rows, width), 0)
    total = jnp.zeros((rows, width), jnp.float32)
    for place, column in enumerate(columns):
        total = jnp.where(lane == row + place * rows, column, total)
    return jnp.sum(total, axis=0, keepdims=True)


def row_to_column(line, place, rows):
    width = line.shape[1]
    lane = lax.broadcasted_iota(jnp.int32, (rows, width), 1)
    row = lax.broadcasted_iota(jnp.int32, (rows, width), 0)
    return jnp.sum(jnp.where(lane == row + place * rows, line, 0.0), axis=1, keepdims=True)


def partners(index, size):
    if size & (size - 1):
        return [index] + [lax.rem(index + k, size) for k in range(1, size)]
    result = []
    for k in range(size):
        value = index
        for bit in range(size.bit_length() - 1):
            if k >> bit & 1:
                value = value + (1 - 2 * lax.rem(lax.div(index, 1 << bit), 2)) * (1 << bit)
        result.append(value)
    return result


def main_kernel(
    sizes,
    hid_hbm, mentor_hbm, w_hbm, mask_hbm,
    wg, hg, div,
    hid, mentor, mask, w, w_other, hsend, held, held_other, h, gx, gx_other, ssend, srecv, part, gsend, grecv,
    hid_sem, mentor_sem, mask_sem, w_sem,
    ws_sem, wr_sem, xs_sem, xr_sem, ts_sem, tr_sem, ss_sem, sr_sem, hs_sem, hr_sem, gs_sem, gr_sem,
):
    nz, nx, nc = sizes
    chips = nz * nx
    sources = nz // nc
    own, depth = hid.shape
    half = own * sources
    rows = half * nc
    vocab = w.shape[0]
    fold = PACK // own
    span = depth // fold
    halves = part.shape[0]
    reach = depth // halves
    unrolled = chips <= 8

    z, x, c = lax.axis_index("vocab"), lax.axis_index("rows"), lax.axis_index("teach")
    place = z * nx + x
    me = place * nc + c
    first = c == 0
    mine_is_source = lax.div(z, sources) == c
    mine_is_owner = lax.div(me, half) == c

    def same_core(step):
        if unrolled:
            zs, xs = partners(z, nz), partners(x, nx)
            for i in reversed(range(1, chips)):
                zz, xx = zs[i // nx], xs[i % nx]
                step(zz * nx + xx, {"vocab": zz, "rows": xx})
            return

        def run(offset, carry):
            d = lax.rem(place + offset, chips)
            step(d, {"vocab": lax.div(d, nx), "rows": lax.rem(d, nx)})
            return carry

        lax.fori_loop(1, chips, run, 0)

    barrier = pltpu.get_barrier_semaphore()

    def greet(at):
        pl.semaphore_signal(barrier, inc=1, device_id=at, device_id_type=pl.DeviceIdType.MESH)

    same_core(lambda d, at: greet(at))
    greet({"teach": 1 - c})

    inputs = [
        pltpu.make_async_copy(hid_hbm, hid, hid_sem),
        pltpu.make_async_copy(mentor_hbm, mentor, mentor_sem),
        pltpu.make_async_copy(mask_hbm, mask, mask_sem),
        pltpu.make_async_copy(w_hbm, w, w_sem),
    ]
    for copy in inputs:
        copy.start()

    inputs[0].wait()
    hidden = hid[...].astype(jnp.float32)
    hsend[...] = jnp.concatenate(
        [hidden[:, k * span:(k + 1) * span] for k in range(fold)], axis=0
    ).astype(jnp.bfloat16)

    pl.semaphore_wait(barrier, chips)

    slot = lax.rem(z, sources)

    @pl.when(mine_is_source)
    def _():
        held[slot] = hsend[...]

        def send_hidden(offset, carry):
            pltpu.make_async_remote_copy(
                src_ref=hsend, dst_ref=held.at[slot], send_sem=hs_sem.at[offset], recv_sem=hr_sem.at[slot],
                device_id={"vocab": lax.rem(z + offset, nz)}, device_id_type=pl.DeviceIdType.MESH,
            ).start()
            return carry

        lax.fori_loop(1, nz, send_hidden, 0, unroll=nz <= 4)

    inputs[3].wait()
    sibling = {"teach": 1 - c}
    w_swap = pltpu.make_async_remote_copy(
        src_ref=w, dst_ref=w_other, send_sem=ws_sem, recv_sem=wr_sem,
        device_id=sibling, device_id_type=pl.DeviceIdType.MESH,
    )
    w_swap.start()

    inputs[1].wait()
    low = mentor[:, :vocab] * (1.0 / smoothing_divisor)
    high = mentor[:, vocab:2 * vocab] * (1.0 / smoothing_divisor)
    scaled = [jnp.where(first, low, high), jnp.where(first, high, low)]

    def largest(pair):
        return jnp.maximum(jnp.max(pair[0], axis=1, keepdims=True), jnp.max(pair[1], axis=1, keepdims=True))

    def added(pair):
        return jnp.sum(pair[0], axis=1, keepdims=True) + jnp.sum(pair[1], axis=1, keepdims=True)

    max_t = largest(scaled)
    weight_t = [jnp.exp(v - max_t) for v in scaled]
    sum_t = added(weight_t)
    part[...] = jnp.zeros_like(part)
    inputs[2].wait()
    keep = row_to_column(mask[...].astype(jnp.float32), c, half)

    for source in range(sources):
        @pl.when(jnp.logical_not(jnp.logical_and(mine_is_source, slot == source)))
        def _():
            pltpu.make_async_copy(hsend, held.at[source], hr_sem.at[source]).wait()

    h_swap = pltpu.make_async_remote_copy(
        src_ref=held, dst_ref=held_other, send_sem=xs_sem, recv_sem=xr_sem,
        device_id=sibling, device_id_type=pl.DeviceIdType.MESH,
    )
    h_swap.start()

    def whole(blocks):
        wide = [blocks[k].astype(jnp.float32) for k in range(sources)]
        return jnp.concatenate(
            [jnp.concatenate([a[k * own:(k + 1) * own] for a in wide], axis=0) for k in range(fold)], axis=1
        )

    mine_h = whole(held)
    mine_b = mine_h.astype(jnp.bfloat16)
    student_own = dot(mine_b, w[...], (1, 1)) * (1.0 / smoothing_divisor)
    w_swap.wait_recv()
    student = [student_own, dot(mine_b, w_other[...], (1, 1)) * (1.0 / smoothing_divisor)]
    max_s = largest(student)
    weight_s = [jnp.exp(v - max_s) for v in student]
    sum_s = added(weight_s)
    cross = added([p * (t - v) for p, t, v in zip(weight_t, scaled, student)])

    width = ssend.shape[1]
    line = column_to_row([max_s, max_t, sum_s, sum_t, cross], width)
    ssend[...] = line
    srecv[place] = line
    same_core(
        lambda d, at: pltpu.make_async_remote_copy(
            src_ref=ssend, dst_ref=srecv.at[place], send_sem=ss_sem, recv_sem=sr_sem,
            device_id=at, device_id_type=pl.DeviceIdType.MESH,
        ).start()
    )
    h_swap.wait_recv()
    theirs_h = whole(held_other)
    h[...] = jnp.concatenate(
        [jnp.where(first, mine_h, theirs_h), jnp.where(first, theirs_h, mine_h)], axis=0
    ).astype(jnp.bfloat16)
    rest = srecv.at[pl.ds(0, chips - 1)]
    pltpu.make_async_copy(rest, rest, sr_sem).wait()
    stats = srecv[:, 0, :]
    top = jnp.max(stats, axis=0, keepdims=True)
    scale = jnp.exp(stats - top)
    lane = lax.broadcasted_iota(jnp.int32, stats.shape, 1)
    scale = jnp.where(lane < 4 * half, pltpu.roll(scale, 2 * half, 1), pltpu.roll(scale, 3 * half, 1))
    sums = jnp.sum(stats * scale, axis=0, keepdims=True)
    all_max_s, all_max_t = row_to_column(top, 0, half), row_to_column(top, 1, half)
    all_sum_s, all_sum_t, all_cross = (row_to_column(sums, k, half) for k in (2, 3, 4))
    lse_s = all_max_s + jnp.log(all_sum_s)
    lse_t = all_max_t + jnp.log(all_sum_t)

    factor = keep * (objective_scale * smoothing_divisor)
    factor_s, factor_t = factor * jnp.exp(max_s - lse_s), factor * jnp.exp(max_t - lse_t)
    grad = [(s * factor_s - t * factor_t).astype(jnp.bfloat16) for s, t in zip(weight_s, weight_t)]

    mine_div = keep * (all_cross / all_sum_t - lse_t + lse_s)
    gx[:, :vocab] = grad[1].astype(jnp.float32)
    gx[:, vocab:vocab + 1] = mine_div
    g_swap = pltpu.make_async_remote_copy(
        src_ref=gx, dst_ref=gx_other, send_sem=ts_sem, recv_sem=tr_sem,
        device_id=sibling, device_id_type=pl.DeviceIdType.MESH,
    )
    g_swap.start()

    for s in range(halves):
        columns = slice(s * reach, (s + 1) * reach)
        term = dot(grad[0], w[:, columns], (1, 0)) + dot(grad[1], w_other[:, columns], (1, 0))
        for k in range(reach // LANES):
            part[s, pl.ds(k, half, stride=PACK), :] = term[:, k * LANES:(k + 1) * LANES]
        gsend[s] = part[s].reshape(half, PACK, LANES).astype(jnp.bfloat16)

        def send_row(r, carry):
            owner = c * half + r

            @pl.when(owner != me)
            def _():
                pltpu.make_async_remote_copy(
                    src_ref=gsend.at[s, r], dst_ref=grecv.at[s, place],
                    send_sem=gs_sem.at[s], recv_sem=gr_sem.at[s],
                    device_id={
                        "vocab": lax.div(owner, nx * nc), "rows": lax.rem(lax.div(owner, nc), nx),
                        "teach": lax.rem(owner, nc),
                    },
                    device_id_type=pl.DeviceIdType.MESH,
                ).start()

            return carry

        lax.fori_loop(0, half, send_row, 0, unroll=unrolled)

        @pl.when(mine_is_owner)
        def _():
            grecv[s, place] = gsend[s, lax.rem(me, half)]

    g_swap.wait_recv()
    theirs = gx_other[:, :vocab]
    own_grad = grad[0].astype(jnp.float32)
    both = jnp.concatenate(
        [jnp.where(first, own_grad, theirs), jnp.where(first, theirs, own_grad)], axis=0
    ).astype(jnp.bfloat16)
    theirs_div = gx_other[:, vocab:vocab + 1]
    div[...] = column_to_row(
        [jnp.where(first, mine_div, theirs_div), jnp.where(first, theirs_div, mine_div)], rows
    )
    step = depth // 7 if depth % (7 * LANES) == 0 else LANES
    for k in range(0, depth, step):
        wg[:, k:k + step] = dot(both, h[:, k:k + step], (0, 0)).astype(jnp.bfloat16)

    def settle(s, sem):
        @pl.when(mine_is_owner)
        def _():
            rest = grecv.at[s, pl.ds(0, chips - 1)]
            pltpu.make_async_copy(rest, rest, sem).wait()

        @pl.when(jnp.logical_not(mine_is_owner))
        def _():
            pltpu.make_async_copy(grecv.at[s], grecv.at[s], sem).wait()

    for s in range(halves):
        settle(s, gr_sem.at[s])
        total = jnp.sum(grecv[s].astype(jnp.float32), axis=0)
        for k in range(reach // LANES):
            at = s * reach + k * LANES
            hg[:, at:at + LANES] = total[k:k + 1].astype(jnp.bfloat16)

    @pl.when(mine_is_source)
    def _():
        def sent(offset, carry):
            pltpu.make_async_copy(hsend, hsend, hs_sem.at[offset]).wait()
            return carry

        lax.fori_loop(1, nz, sent, 0)

    for swap in (w_swap, h_swap, g_swap):
        swap.wait_send()
    rest = srecv.at[pl.ds(0, chips - 1)]
    pltpu.make_async_copy(rest, rest, ss_sem).wait()
    for s in range(halves):
        settle(s, gs_sem.at[s])


def write_kernel(wg, hg, div, wg_out, hg_out, div_out, wg_sem, hg_sem, div_sem):
    vocab = wg.shape[0]
    slab = -(-vocab // (wg_sem.shape[0] * PACK)) * PACK
    copies = [pltpu.make_async_copy(hg, hg_out, hg_sem), pltpu.make_async_copy(div, div_out, div_sem)]
    for k, first in enumerate(range(0, vocab, slab)):
        at = pl.ds(first, min(slab, vocab - first))
        copies.append(pltpu.make_async_copy(wg.at[at], wg_out.at[at], wg_sem.at[k]))
    for copy in copies:
        copy.start()
    for copy in copies:
        copy.wait()


def body(sizes, hidden_rows, mentor_unnormalized, head_weight, row_mask):
    nz, nx, nc = sizes
    n = nz * nx * nc
    own, depth = hidden_rows.shape
    vocab = head_weight.shape[0]
    rows = own * nz
    half = mentor_unnormalized.shape[0]
    assert rows == n and nc == 2 and nz % nc == 0 and half == rows // nc
    assert PACK % own == 0 and depth % (PACK // own * LANES) == 0
    fold = PACK // own
    chips = nz * nx
    sources = nz // nc
    span = depth // fold
    halves = 2
    assert depth % (halves * LANES) == 0 and depth // (halves * LANES) <= PACK
    wide = -(-(vocab + 1) // LANES) * LANES
    width = -(-5 * half // LANES) * LANES
    vmem = pl.BlockSpec(memory_space=pltpu.VMEM)
    hbm = pl.BlockSpec(memory_space=pltpu.HBM)
    dma = pltpu.SemaphoreType.DMA
    results = (
        jax.ShapeDtypeStruct((vocab, depth), jnp.bfloat16),
        jax.ShapeDtypeStruct((1, depth), jnp.bfloat16),
        jax.ShapeDtypeStruct((1, rows), jnp.float32),
    )
    made = pl.pallas_call(
        functools.partial(main_kernel, sizes),
        out_shape=results,
        in_specs=[hbm, hbm, hbm, hbm],
        out_specs=(vmem, vmem, vmem),
        scratch_shapes=[
            pltpu.VMEM((own, depth), jnp.bfloat16),
            pltpu.VMEM(mentor_unnormalized.shape, jnp.float32),
            pltpu.VMEM((1, rows), jnp.int32),
            pltpu.VMEM((vocab, depth), jnp.bfloat16),
            pltpu.VMEM((vocab, depth), jnp.bfloat16),
            pltpu.VMEM((PACK, span), jnp.bfloat16),
            pltpu.VMEM((sources, PACK, span), jnp.bfloat16),
            pltpu.VMEM((sources, PACK, span), jnp.bfloat16),
            pltpu.VMEM((rows, depth), jnp.bfloat16),
            pltpu.VMEM((half, wide), jnp.float32),
            pltpu.VMEM((half, wide), jnp.float32),
            pltpu.VMEM((1, width), jnp.float32),
            pltpu.VMEM((chips, 1, width), jnp.float32),
            pltpu.VMEM((halves, half * PACK, LANES), jnp.float32),
            pltpu.VMEM((halves, half, PACK, LANES), jnp.bfloat16),
            pltpu.VMEM((halves, chips, PACK, LANES), jnp.bfloat16),
        ] + [dma] * 12 + [dma((nz,)), dma((sources,))] + [dma((halves,))] * 2,
        compiler_params=pltpu.CompilerParams(
            collective_id=0, has_side_effects=True, vmem_limit_bytes=44 * 2**20
        ),
    )(*(
        pltpu.with_memory_space_constraint(a, pltpu.HBM)
        for a in (hidden_rows, mentor_unnormalized, head_weight, row_mask.reshape(1, rows))
    ))
    wg, hg, div = pl.pallas_call(
        write_kernel,
        out_shape=results,
        in_specs=[vmem, vmem, vmem],
        out_specs=(hbm, hbm, hbm),
        scratch_shapes=[dma((4,)), dma, dma],
        compiler_params=pltpu.CompilerParams(vmem_limit_bytes=4 * 2**20),
    )(*(pltpu.with_memory_space_constraint(a, pltpu.VMEM) for a in made))
    return div.reshape(rows), hg, wg


def solution(mesh):
    sizes = (mesh.shape["vocab"], mesh.shape["rows"], mesh.shape["teach"])
    return jax.shard_map(
        functools.partial(body, sizes),
        mesh=mesh,
        in_specs=(
            P(("groups", "vocab"), None),
            P(("groups", "teach"), ("vocab", "rows")),
            P(("vocab", "rows", "teach"), None),
            P("groups"),
        ),
        out_specs=(
            P("groups"),
            P(("groups", "vocab", "rows", "teach"), None),
            P(("groups", "vocab", "rows", "teach"), None),
        ),
        check_vma=False,
    )
```

```python
import functools

import jax
import jax.numpy as jnp
from jax import lax
from jax.experimental import pallas as pl
from jax.experimental.pallas import tpu as pltpu
from jax.sharding import PartitionSpec as P

smoothing_divisor = 2.0
objective_scale = 256.0

LANES = 128
PACK = 16


def dot(a, b, contract):
    return lax.dot_general(a, b, ((contract[:1], contract[1:]), ((), ())), preferred_element_type=jnp.float32)


def column_to_row(columns, width):
    rows = columns[0].shape[0]
    lane = lax.broadcasted_iota(jnp.int32, (rows, width), 1)
    row = lax.broadcasted_iota(jnp.int32, (rows, width), 0)
    total = jnp.zeros((rows, width), jnp.float32)
    for place, column in enumerate(columns):
        total = jnp.where(lane == row + place * rows, column, total)
    return jnp.sum(total, axis=0, keepdims=True)


def row_to_column(line, place, rows):
    width = line.shape[1]
    lane = lax.broadcasted_iota(jnp.int32, (rows, width), 1)
    row = lax.broadcasted_iota(jnp.int32, (rows, width), 0)
    return jnp.sum(jnp.where(lane == row + place * rows, line, 0.0), axis=1, keepdims=True)


def partners(index, size):
    if size & (size - 1):
        return [index] + [lax.rem(index + k, size) for k in range(1, size)]
    result = []
    for k in range(size):
        value = index
        for bit in range(size.bit_length() - 1):
            if k >> bit & 1:
                value = value + (1 - 2 * lax.rem(lax.div(index, 1 << bit), 2)) * (1 << bit)
        result.append(value)
    return result


def main_kernel(
    sizes,
    hid_hbm, mentor_hbm, w_hbm, mask_hbm,
    wg, hg, div,
    hid, mentor, mask, w, hsend, direct, relayed, h, tsend, trecv, ssend, srecv, part, theirs_part, gsend, grecv,
    hid_sem, mentor_sem, mask_sem, w_sem,
    hs_sem, rs_sem, rr_sem, ts_sem, tr_sem, ss_sem, sr_sem, hr_sem, ps_sem, pr_sem, gs_sem, gr_sem,
):
    nz, nx, nc = sizes
    n = nz * nx * nc
    own, depth = hid.shape
    rows = own * nz
    vocab = w.shape[0]
    fold = PACK // own
    span = depth // fold
    halves = part.shape[0]
    reach = depth // halves
    unrolled = n <= 16

    z, x, c = lax.axis_index("vocab"), lax.axis_index("rows"), lax.axis_index("teach")
    me = (z * nx + x) * nc + c

    def others(step):
        if unrolled:
            zs, xs, cs = partners(z, nz), partners(x, nx), partners(c, nc)
            for i in reversed(range(1, n)):
                zz, xx, cc = zs[i // (nx * nc)], xs[i // nc % nx], cs[i % nc]
                step((zz * nx + xx) * nc + cc, {"vocab": zz, "rows": xx, "teach": cc})
            return

        def run(offset, carry):
            d = lax.rem(me + offset, n)
            step(d, {
                "vocab": lax.div(d, nx * nc), "rows": lax.rem(lax.div(d, nc), nx), "teach": lax.rem(d, nc),
            })
            return carry

        lax.fori_loop(1, n, run, 0)

    def same_core(step):
        if unrolled:
            zs, xs = partners(z, nz), partners(x, nx)
            for i in reversed(range(1, nz * nx)):
                zz, xx = zs[i // nx], xs[i % nx]
                step(zz * nx + xx, {"vocab": zz, "rows": xx})
            return

        def run(offset, carry):
            d = lax.rem(z * nx + x + offset, nz * nx)
            step(d, {"vocab": lax.div(d, nx), "rows": lax.rem(d, nx)})
            return carry

        lax.fori_loop(1, nz * nx, run, 0)

    barrier = pltpu.get_barrier_semaphore()

    def greet(at):
        pl.semaphore_signal(barrier, inc=1, device_id=at, device_id_type=pl.DeviceIdType.MESH)

    def greet_line(offset, carry):
        greet({"vocab": lax.rem(z + offset, nz)})
        return carry

    lax.fori_loop(1, nz, greet_line, 0, unroll=nz <= 4)
    for i in range(1, nx * nc):
        greet({"rows": lax.rem(x + i // nc, nx), "teach": lax.rem(c + i % nc, nc)})

    inputs = [
        pltpu.make_async_copy(hid_hbm, hid, hid_sem),
        pltpu.make_async_copy(mentor_hbm, mentor, mentor_sem),
        pltpu.make_async_copy(mask_hbm, mask, mask_sem),
        pltpu.make_async_copy(w_hbm, w, w_sem),
    ]
    for copy in inputs:
        copy.start()

    first = c == 0
    piece = direct.shape[2]
    rest_of = span - piece
    inputs[0].wait()
    hidden = hid[...].astype(jnp.float32)
    packed = jnp.concatenate([hidden[:, k * span:(k + 1) * span] for k in range(fold)], axis=0).astype(jnp.bfloat16)
    low, high = packed[:, :piece], packed[:, rest_of:]
    hsend[...] = jnp.where(first, low, high)
    direct[z] = jnp.where(first, low, high)
    relayed[z] = jnp.where(first, high, low)

    pl.semaphore_wait(barrier, nz - 1 + nx * nc - 1)

    def send_hidden(to):
        pltpu.make_async_remote_copy(
            src_ref=hsend, dst_ref=direct.at[z], send_sem=hs_sem, recv_sem=hr_sem.at[z],
            device_id={"vocab": to}, device_id_type=pl.DeviceIdType.MESH,
        ).start()

    def relay(source):
        pltpu.make_async_copy(hsend, direct.at[source], hr_sem.at[source]).wait()
        pltpu.make_async_remote_copy(
            src_ref=direct.at[source], dst_ref=relayed.at[source], send_sem=rs_sem, recv_sem=rr_sem,
            device_id={"teach": 1 - c}, device_id_type=pl.DeviceIdType.MESH,
        ).start()

    def line(step, far_first):
        if unrolled:
            peers = partners(z, nz)[1:]
            for zz in reversed(peers) if far_first else peers:
                step(zz)
            return

        def run(offset, carry):
            step(lax.rem(z + offset, nz))
            return carry

        lax.fori_loop(1, nz, run, 0)

    line(send_hidden, True)

    inputs[1].wait()
    low = mentor[:, :vocab]
    high = mentor[:, vocab:2 * vocab]
    mine = jnp.where(first, low, high)
    tsend[:, :vocab] = jnp.where(first, high, low)
    teacher_copy = pltpu.make_async_remote_copy(
        src_ref=tsend, dst_ref=trecv, send_sem=ts_sem, recv_sem=tr_sem,
        device_id={"teach": 1 - c}, device_id_type=pl.DeviceIdType.MESH,
    )
    teacher_copy.start()
    part[...] = jnp.zeros_like(part)
    inputs[2].wait()
    keep = row_to_column(mask[...].astype(jnp.float32), 0, rows)

    line(relay, False)

    teacher_copy.wait_recv()
    theirs = trecv[:, :vocab]
    scaled = jnp.concatenate(
        [jnp.where(first, mine, theirs), jnp.where(first, theirs, mine)], axis=0
    ) * (1.0 / smoothing_divisor)
    max_t = jnp.max(scaled, axis=1, keepdims=True)
    weight_t = jnp.exp(scaled - max_t)
    sum_t = jnp.sum(weight_t, axis=1, keepdims=True)

    inputs[3].wait()

    def columns_of(held, k, start, width):
        return jnp.concatenate(
            [held[zz, :, pl.ds(start, width)][k * own:(k + 1) * own].astype(jnp.float32) for zz in range(nz)], axis=0
        ).astype(jnp.bfloat16)

    logits = jnp.zeros((rows, vocab), jnp.float32)
    for k in range(fold):
        at = pl.multiple_of(k * span + c * rest_of, LANES)
        logits += dot(columns_of(direct, k, 0, piece), w[:, pl.ds(at, piece)], (1, 1))
    peers = relayed.at[pl.ds(0, nz - 1)]
    pltpu.make_async_copy(peers, peers, rr_sem).wait()
    for k in range(fold):
        start = pl.multiple_of((1 - c) * (piece - rest_of), LANES)
        at = pl.multiple_of(k * span + (1 - c) * piece, LANES)
        logits += dot(columns_of(relayed, k, start, rest_of), w[:, pl.ds(at, rest_of)], (1, 1))

    student = logits * (1.0 / smoothing_divisor)
    max_s = jnp.max(student, axis=1, keepdims=True)
    weight_s = jnp.exp(student - max_s)
    sum_s = jnp.sum(weight_s, axis=1, keepdims=True)
    cross = jnp.sum(weight_t * (scaled - student), axis=1, keepdims=True)

    width = ssend.shape[1]
    line = column_to_row([max_s, max_t, sum_s, sum_t, cross], width)
    ssend[...] = line
    srecv[me] = line
    others(
        lambda d, at: pltpu.make_async_remote_copy(
            src_ref=ssend, dst_ref=srecv.at[me], send_sem=ss_sem, recv_sem=sr_sem,
            device_id=at, device_id_type=pl.DeviceIdType.MESH,
        ).start()
    )
    arrived = []
    for k in range(nz):
        low = jnp.where(first, direct[k], relayed[k])
        high = jnp.where(first, relayed[k], direct[k])
        arrived.append(jnp.concatenate([low, high[:, piece - rest_of:]], axis=1).astype(jnp.float32))
    for k in range(fold):
        h[:, k * span:(k + 1) * span] = jnp.concatenate(
            [a[k * own:(k + 1) * own] for a in arrived], axis=0
        ).astype(jnp.bfloat16)
    pltpu.make_async_copy(srecv.at[pl.ds(0, n - 1)], srecv.at[pl.ds(0, n - 1)], sr_sem).wait()
    stats = srecv[:, 0, :]
    top = jnp.max(stats, axis=0, keepdims=True)
    scale = jnp.exp(stats - top)
    lane = lax.broadcasted_iota(jnp.int32, stats.shape, 1)
    scale = jnp.where(lane < 4 * rows, pltpu.roll(scale, 2 * rows, 1), pltpu.roll(scale, 3 * rows, 1))
    sums = jnp.sum(stats * scale, axis=0, keepdims=True)
    all_max_s, all_max_t = row_to_column(top, 0, rows), row_to_column(top, 1, rows)
    all_sum_s, all_sum_t, all_cross = (row_to_column(sums, k, rows) for k in (2, 3, 4))
    lse_s = all_max_s + jnp.log(all_sum_s)
    lse_t = all_max_t + jnp.log(all_sum_t)

    factor = keep * (objective_scale * smoothing_divisor)
    grad = (
        weight_s * (factor * jnp.exp(max_s - lse_s)) - weight_t * (factor * jnp.exp(max_t - lse_t))
    ).astype(jnp.bfloat16)

    chips = nz * nx
    place = z * nx + x
    swaps = []
    for s in range(halves):
        term = dot(grad, w[:, s * reach:(s + 1) * reach], (1, 0))
        for k in range(reach // LANES):
            part[s, pl.ds(k, rows, stride=PACK), :] = term[:, k * LANES:(k + 1) * LANES]
        swaps.append(pltpu.make_async_remote_copy(
            src_ref=part.at[s].reshape(chips, nc, PACK, LANES).at[:, 1 - c], dst_ref=theirs_part.at[s],
            send_sem=ps_sem.at[s], recv_sem=pr_sem.at[s],
            device_id={"teach": 1 - c}, device_id_type=pl.DeviceIdType.MESH,
        ))
        swaps[-1].start()
    step = depth // 14 if depth % (14 * LANES) == 0 else LANES
    steps = range(0, depth, step)
    early = len(steps) // 5

    def weight_grad(k):
        wg[:, k:k + step] = dot(grad, h[:, k:k + step], (0, 0)).astype(jnp.bfloat16)

    for s in range(halves):
        for k in steps[s * early:(s + 1) * early]:
            weight_grad(k)
        swaps[s].wait_recv()
        both = part[s].reshape(chips, nc, PACK, LANES)
        own_part = jnp.where(first, both[:, 0], both[:, 1])
        gsend[s] = (own_part + theirs_part[s]).astype(jnp.bfloat16)
        same_core(
            lambda d, at: pltpu.make_async_remote_copy(
                src_ref=gsend.at[s, d], dst_ref=grecv.at[s, place],
                send_sem=gs_sem.at[s], recv_sem=gr_sem.at[s],
                device_id=at, device_id_type=pl.DeviceIdType.MESH,
            ).start()
        )
        grecv[s, place] = gsend[s, place]

    div[...] = column_to_row([keep * (all_cross / all_sum_t - lse_t + lse_s)], rows)
    for k in steps[2 * early:]:
        weight_grad(k)

    for s in range(halves):
        rest = grecv.at[s, pl.ds(0, chips - 1)]
        pltpu.make_async_copy(rest, rest, gr_sem.at[s]).wait()
        total = jnp.sum(grecv[s].astype(jnp.float32), axis=0)
        for k in range(reach // LANES):
            at = s * reach + k * LANES
            hg[:, at:at + LANES] = total[k:k + 1].astype(jnp.bfloat16)

    pltpu.make_async_copy(peers, peers, hs_sem).wait()
    pltpu.make_async_copy(peers, peers, rs_sem).wait()
    teacher_copy.wait_send()
    for swap in swaps:
        swap.wait_send()
    pltpu.make_async_copy(srecv.at[pl.ds(0, n - 1)], srecv.at[pl.ds(0, n - 1)], ss_sem).wait()
    for s in range(halves):
        rest = grecv.at[s, pl.ds(0, chips - 1)]
        pltpu.make_async_copy(rest, rest, gs_sem.at[s]).wait()


def write_kernel(wg, hg, div, wg_out, hg_out, div_out, wg_sem, hg_sem, div_sem):
    vocab = wg.shape[0]
    slab = -(-vocab // (wg_sem.shape[0] * PACK)) * PACK
    copies = [pltpu.make_async_copy(hg, hg_out, hg_sem), pltpu.make_async_copy(div, div_out, div_sem)]
    for k, first in enumerate(range(0, vocab, slab)):
        at = pl.ds(first, min(slab, vocab - first))
        copies.append(pltpu.make_async_copy(wg.at[at], wg_out.at[at], wg_sem.at[k]))
    for copy in copies:
        copy.start()
    for copy in copies:
        copy.wait()


def body(sizes, hidden_rows, mentor_unnormalized, head_weight, row_mask):
    nz, nx, nc = sizes
    n = nz * nx * nc
    own, depth = hidden_rows.shape
    vocab = head_weight.shape[0]
    rows = own * nz
    half = mentor_unnormalized.shape[0]
    assert rows == n and nc == 2 and PACK % own == 0
    fold = PACK // own
    assert depth % (fold * LANES) == 0
    piece = -(-depth // (fold * nc * LANES)) * LANES
    halves = 2
    assert depth % (halves * LANES) == 0 and depth // (halves * LANES) <= PACK
    wide = -(-vocab // LANES) * LANES
    width = -(-5 * rows // LANES) * LANES
    vmem = pl.BlockSpec(memory_space=pltpu.VMEM)
    hbm = pl.BlockSpec(memory_space=pltpu.HBM)
    dma = pltpu.SemaphoreType.DMA
    results = (
        jax.ShapeDtypeStruct((vocab, depth), jnp.bfloat16),
        jax.ShapeDtypeStruct((1, depth), jnp.bfloat16),
        jax.ShapeDtypeStruct((1, rows), jnp.float32),
    )
    made = pl.pallas_call(
        functools.partial(main_kernel, sizes),
        out_shape=results,
        in_specs=[hbm, hbm, hbm, hbm],
        out_specs=(vmem, vmem, vmem),
        scratch_shapes=[
            pltpu.VMEM((own, depth), jnp.bfloat16),
            pltpu.VMEM(mentor_unnormalized.shape, jnp.float32),
            pltpu.VMEM((1, rows), jnp.int32),
            pltpu.VMEM((vocab, depth), jnp.bfloat16),
            pltpu.VMEM((PACK, piece), jnp.bfloat16),
            pltpu.VMEM((nz, PACK, piece), jnp.bfloat16),
            pltpu.VMEM((nz, PACK, piece), jnp.bfloat16),
            pltpu.VMEM((rows, depth), jnp.bfloat16),
            pltpu.VMEM((half, wide), jnp.float32),
            pltpu.VMEM((half, wide), jnp.float32),
            pltpu.VMEM((1, width), jnp.float32),
            pltpu.VMEM((n, 1, width), jnp.float32),
            pltpu.VMEM((halves, rows * PACK, LANES), jnp.float32),
            pltpu.VMEM((halves, rows // nc, PACK, LANES), jnp.float32),
            pltpu.VMEM((halves, rows // nc, PACK, LANES), jnp.bfloat16),
            pltpu.VMEM((halves, rows // nc, PACK, LANES), jnp.bfloat16),
        ] + [dma] * 11 + [dma((nz,))] + [dma((halves,))] * 4,
        compiler_params=pltpu.CompilerParams(
            collective_id=0, has_side_effects=True, vmem_limit_bytes=44 * 2**20
        ),
    )(*(
        pltpu.with_memory_space_constraint(a, pltpu.HBM)
        for a in (hidden_rows, mentor_unnormalized, head_weight, row_mask.reshape(1, rows))
    ))
    wg, hg, div = pl.pallas_call(
        write_kernel,
        out_shape=results,
        in_specs=[vmem, vmem, vmem],
        out_specs=(hbm, hbm, hbm),
        scratch_shapes=[dma((4,)), dma, dma],
        compiler_params=pltpu.CompilerParams(vmem_limit_bytes=4 * 2**20),
    )(*(pltpu.with_memory_space_constraint(a, pltpu.VMEM) for a in made))
    return div.reshape(rows), hg, wg


def solution(mesh):
    sizes = (mesh.shape["vocab"], mesh.shape["rows"], mesh.shape["teach"])
    return jax.shard_map(
        functools.partial(body, sizes),
        mesh=mesh,
        in_specs=(
            P(("groups", "vocab"), None),
            P(("groups", "teach"), ("vocab", "rows")),
            P(("vocab", "rows", "teach"), None),
            P("groups"),
        ),
        out_specs=(
            P("groups"),
            P(("groups", "vocab", "rows", "teach"), None),
            P(("groups", "vocab", "rows", "teach"), None),
        ),
        check_vma=False,
    )
```

```python
import functools

import jax
import jax.numpy as jnp
from jax import lax
from jax.experimental import pallas as pl
from jax.experimental.pallas import tpu as pltpu
from jax.sharding import PartitionSpec as P

smoothing_divisor = 2.0
objective_scale = 256.0

LANES = 128
PACK = 16


def dot(a, b, contract):
    return lax.dot_general(a, b, ((contract[:1], contract[1:]), ((), ())), preferred_element_type=jnp.float32)


def column_to_row(columns, width):
    rows = columns[0].shape[0]
    lane = lax.broadcasted_iota(jnp.int32, (rows, width), 1)
    row = lax.broadcasted_iota(jnp.int32, (rows, width), 0)
    total = jnp.zeros((rows, width), jnp.float32)
    for place, column in enumerate(columns):
        total = jnp.where(lane == row + place * rows, column, total)
    return jnp.sum(total, axis=0, keepdims=True)


def row_to_column(line, place, rows):
    width = line.shape[1]
    lane = lax.broadcasted_iota(jnp.int32, (rows, width), 1)
    row = lax.broadcasted_iota(jnp.int32, (rows, width), 0)
    return jnp.sum(jnp.where(lane == row + place * rows, line, 0.0), axis=1, keepdims=True)


def partners(index, size):
    if size & (size - 1):
        return [index] + [lax.rem(index + k, size) for k in range(1, size)]
    result = []
    for k in range(size):
        value = index
        for bit in range(size.bit_length() - 1):
            if k >> bit & 1:
                value = value + (1 - 2 * lax.rem(lax.div(index, 1 << bit), 2)) * (1 << bit)
        result.append(value)
    return result


def flipped(index, k, size):
    if size & (size - 1):
        return lax.rem(index + k, size)
    value = index
    for bit in range(size.bit_length() - 1):
        has, flip = (lax.rem(lax.div(v, 1 << bit), 2) for v in (index, k))
        value = value + flip * (1 - 2 * has) * (1 << bit)
    return value


def main_kernel(
    sizes,
    hid_hbm, mentor_hbm, w_hbm, mask_hbm,
    wg, hg, div,
    hid, mentor, mask, w, hsend, direct, relayed, h, tsend, trecv, ssend, srecv, part, theirs_part, gsend, grecv,
    hid_sem, mentor_sem, mask_sem, w_sem,
    hs_sem, rs_sem, rr_sem, ts_sem, tr_sem, ss_sem, sr_sem, hr_sem, ps_sem, pr_sem, gs_sem, gr_sem,
):
    nz, nx, nc = sizes
    n = nz * nx * nc
    own, depth = hid.shape
    rows = own * nz
    vocab = w.shape[0]
    fold = PACK // own
    span = depth // fold
    halves = part.shape[0]
    reach = depth // halves
    unrolled = n <= 16

    z, x, c = lax.axis_index("vocab"), lax.axis_index("rows"), lax.axis_index("teach")
    me = (z * nx + x) * nc + c

    def others(step):
        def run(i, carry):
            d = flipped(me, n - 1 - i, n)
            step(d, {
                "vocab": lax.div(d, nx * nc), "rows": lax.rem(lax.div(d, nc), nx), "teach": lax.rem(d, nc),
            })
            return carry

        lax.fori_loop(0, n - 1, run, 0)

    def same_core(step):
        def run(i, carry):
            d = flipped(z * nx + x, nz * nx - 1 - i, nz * nx)
            step(d, {"vocab": lax.div(d, nx), "rows": lax.rem(d, nx)})
            return carry

        lax.fori_loop(0, nz * nx - 1, run, 0)

    barrier = pltpu.get_barrier_semaphore()

    def greet(at):
        pl.semaphore_signal(barrier, inc=1, device_id=at, device_id_type=pl.DeviceIdType.MESH)

    def greet_line(offset, carry):
        greet({"vocab": lax.rem(z + offset, nz)})
        return carry

    lax.fori_loop(1, nz, greet_line, 0, unroll=nz <= 4)
    for i in range(1, nx * nc):
        greet({"rows": lax.rem(x + i // nc, nx), "teach": lax.rem(c + i % nc, nc)})

    inputs = [
        pltpu.make_async_copy(hid_hbm, hid, hid_sem),
        pltpu.make_async_copy(mentor_hbm, mentor, mentor_sem),
        pltpu.make_async_copy(mask_hbm, mask, mask_sem),
        pltpu.make_async_copy(w_hbm, w, w_sem),
    ]
    for copy in inputs:
        copy.start()

    first = c == 0
    piece = direct.shape[2]
    rest_of = span - piece
    inputs[0].wait()
    hidden = hid[...].astype(jnp.float32)
    packed = jnp.concatenate([hidden[:, k * span:(k + 1) * span] for k in range(fold)], axis=0).astype(jnp.bfloat16)
    low, high = packed[:, :piece], packed[:, rest_of:]
    hsend[...] = jnp.where(first, low, high)
    direct[z] = jnp.where(first, low, high)
    relayed[z] = jnp.where(first, high, low)

    pl.semaphore_wait(barrier, nz - 1 + nx * nc - 1)

    def send_hidden(to):
        pltpu.make_async_remote_copy(
            src_ref=hsend, dst_ref=direct.at[z], send_sem=hs_sem, recv_sem=hr_sem.at[z],
            device_id={"vocab": to}, device_id_type=pl.DeviceIdType.MESH,
        ).start()

    def relay(source):
        pltpu.make_async_copy(hsend, direct.at[source], hr_sem.at[source]).wait()
        pltpu.make_async_remote_copy(
            src_ref=direct.at[source], dst_ref=relayed.at[source], send_sem=rs_sem, recv_sem=rr_sem,
            device_id={"teach": 1 - c}, device_id_type=pl.DeviceIdType.MESH,
        ).start()

    def line(step, far_first):
        if unrolled:
            peers = partners(z, nz)[1:]
            for zz in reversed(peers) if far_first else peers:
                step(zz)
            return

        def run(offset, carry):
            step(lax.rem(z + offset, nz))
            return carry

        lax.fori_loop(1, nz, run, 0)

    line(send_hidden, True)

    inputs[1].wait()
    low = mentor[:, :vocab]
    high = mentor[:, vocab:2 * vocab]
    mine = jnp.where(first, low, high)
    tsend[:, :vocab] = jnp.where(first, high, low)
    teacher_copy = pltpu.make_async_remote_copy(
        src_ref=tsend, dst_ref=trecv, send_sem=ts_sem, recv_sem=tr_sem,
        device_id={"teach": 1 - c}, device_id_type=pl.DeviceIdType.MESH,
    )
    teacher_copy.start()
    part[...] = jnp.zeros_like(part)
    inputs[2].wait()
    keep = row_to_column(mask[...].astype(jnp.float32), 0, rows)

    line(relay, False)

    teacher_copy.wait_recv()
    theirs = trecv[:, :vocab]
    scaled = jnp.concatenate(
        [jnp.where(first, mine, theirs), jnp.where(first, theirs, mine)], axis=0
    ) * (1.0 / smoothing_divisor)
    max_t = jnp.max(scaled, axis=1, keepdims=True)
    weight_t = jnp.exp(scaled - max_t)
    sum_t = jnp.sum(weight_t, axis=1, keepdims=True)

    inputs[3].wait()

    def columns_of(held, k, start, width):
        return jnp.concatenate(
            [held[zz, :, pl.ds(start, width)][k * own:(k + 1) * own].astype(jnp.float32) for zz in range(nz)], axis=0
        ).astype(jnp.bfloat16)

    logits = jnp.zeros((rows, vocab), jnp.float32)
    for k in range(fold):
        at = pl.multiple_of(k * span + c * rest_of, LANES)
        logits += dot(columns_of(direct, k, 0, piece), w[:, pl.ds(at, piece)], (1, 1))
    peers = relayed.at[pl.ds(0, nz - 1)]
    pltpu.make_async_copy(peers, peers, rr_sem).wait()
    for k in range(fold):
        start = pl.multiple_of((1 - c) * (piece - rest_of), LANES)
        at = pl.multiple_of(k * span + (1 - c) * piece, LANES)
        logits += dot(columns_of(relayed, k, start, rest_of), w[:, pl.ds(at, rest_of)], (1, 1))

    student = logits * (1.0 / smoothing_divisor)
    max_s = jnp.max(student, axis=1, keepdims=True)
    weight_s = jnp.exp(student - max_s)
    sum_s = jnp.sum(weight_s, axis=1, keepdims=True)
    cross = jnp.sum(weight_t * (scaled - student), axis=1, keepdims=True)

    width = ssend.shape[1]
    line = column_to_row([max_s, max_t, sum_s, sum_t, cross], width)
    ssend[...] = line
    srecv[me] = line
    others(
        lambda d, at: pltpu.make_async_remote_copy(
            src_ref=ssend, dst_ref=srecv.at[me], send_sem=ss_sem, recv_sem=sr_sem,
            device_id=at, device_id_type=pl.DeviceIdType.MESH,
        ).start()
    )
    arrived = []
    for k in range(nz):
        low = jnp.where(first, direct[k], relayed[k])
        high = jnp.where(first, relayed[k], direct[k])
        arrived.append(jnp.concatenate([low, high[:, piece - rest_of:]], axis=1).astype(jnp.float32))
    for k in range(fold):
        h[:, k * span:(k + 1) * span] = jnp.concatenate(
            [a[k * own:(k + 1) * own] for a in arrived], axis=0
        ).astype(jnp.bfloat16)
    pltpu.make_async_copy(srecv.at[pl.ds(0, n - 1)], srecv.at[pl.ds(0, n - 1)], sr_sem).wait()
    stats = srecv[:, 0, :]
    top = jnp.max(stats, axis=0, keepdims=True)
    scale = jnp.exp(stats - top)
    lane = lax.broadcasted_iota(jnp.int32, stats.shape, 1)
    scale = jnp.where(lane < 4 * rows, pltpu.roll(scale, 2 * rows, 1), pltpu.roll(scale, 3 * rows, 1))
    sums = jnp.sum(stats * scale, axis=0, keepdims=True)
    all_max_s, all_max_t = row_to_column(top, 0, rows), row_to_column(top, 1, rows)
    all_sum_s, all_sum_t, all_cross = (row_to_column(sums, k, rows) for k in (2, 3, 4))
    lse_s = all_max_s + jnp.log(all_sum_s)
    lse_t = all_max_t + jnp.log(all_sum_t)

    factor = keep * (objective_scale * smoothing_divisor)
    grad = (
        weight_s * (factor * jnp.exp(max_s - lse_s)) - weight_t * (factor * jnp.exp(max_t - lse_t))
    ).astype(jnp.bfloat16)

    chips = nz * nx
    place = z * nx + x
    swaps = []
    for s in range(halves):
        term = dot(grad, w[:, s * reach:(s + 1) * reach], (1, 0))
        for k in range(reach // LANES):
            part[s, pl.ds(k, rows, stride=PACK), :] = term[:, k * LANES:(k + 1) * LANES]
        swaps.append(pltpu.make_async_remote_copy(
            src_ref=part.at[s].reshape(chips, nc, PACK, LANES).at[:, 1 - c], dst_ref=theirs_part.at[s],
            send_sem=ps_sem.at[s], recv_sem=pr_sem.at[s],
            device_id={"teach": 1 - c}, device_id_type=pl.DeviceIdType.MESH,
        ))
        swaps[-1].start()
    step = depth // 14 if depth % (14 * LANES) == 0 else LANES
    early = depth // step // 5

    grad_t = grad.astype(jnp.float32).T.astype(jnp.bfloat16)

    def weight_grad(i, carry):
        at = pl.ds(pl.multiple_of(i * step, step), step)
        wg[:, at] = dot(grad_t, h[:, at], (1, 0)).astype(jnp.bfloat16)
        return carry

    for s in range(halves):
        lax.fori_loop(s * early, (s + 1) * early, weight_grad, 0)
        swaps[s].wait_recv()
        both = part[s].reshape(chips, nc, PACK, LANES)
        own_part = jnp.where(first, both[:, 0], both[:, 1])
        gsend[s] = (own_part + theirs_part[s]).astype(jnp.bfloat16)
        same_core(
            lambda d, at: pltpu.make_async_remote_copy(
                src_ref=gsend.at[s, d], dst_ref=grecv.at[s, place],
                send_sem=gs_sem.at[s], recv_sem=gr_sem.at[s],
                device_id=at, device_id_type=pl.DeviceIdType.MESH,
            ).start()
        )
        grecv[s, place] = gsend[s, place]

    div[...] = column_to_row([keep * (all_cross / all_sum_t - lse_t + lse_s)], rows)
    lax.fori_loop(halves * early, depth // step, weight_grad, 0)

    for s in range(halves):
        rest = grecv.at[s, pl.ds(0, chips - 1)]
        pltpu.make_async_copy(rest, rest, gr_sem.at[s]).wait()
        total = jnp.sum(grecv[s].astype(jnp.float32), axis=0)
        for k in range(reach // LANES):
            at = s * reach + k * LANES
            hg[:, at:at + LANES] = total[k:k + 1].astype(jnp.bfloat16)

    pltpu.make_async_copy(peers, peers, hs_sem).wait()
    pltpu.make_async_copy(peers, peers, rs_sem).wait()
    teacher_copy.wait_send()
    for swap in swaps:
        swap.wait_send()
    pltpu.make_async_copy(srecv.at[pl.ds(0, n - 1)], srecv.at[pl.ds(0, n - 1)], ss_sem).wait()
    for s in range(halves):
        rest = grecv.at[s, pl.ds(0, chips - 1)]
        pltpu.make_async_copy(rest, rest, gs_sem.at[s]).wait()


def write_kernel(wg, hg, div, wg_out, hg_out, div_out, wg_sem, hg_sem, div_sem):
    vocab = wg.shape[0]
    slab = -(-vocab // (wg_sem.shape[0] * PACK)) * PACK
    copies = [pltpu.make_async_copy(hg, hg_out, hg_sem), pltpu.make_async_copy(div, div_out, div_sem)]
    for k, first in enumerate(range(0, vocab, slab)):
        at = pl.ds(first, min(slab, vocab - first))
        copies.append(pltpu.make_async_copy(wg.at[at], wg_out.at[at], wg_sem.at[k]))
    for copy in copies:
        copy.start()
    for copy in copies:
        copy.wait()


def body(sizes, hidden_rows, mentor_unnormalized, head_weight, row_mask):
    nz, nx, nc = sizes
    n = nz * nx * nc
    own, depth = hidden_rows.shape
    vocab = head_weight.shape[0]
    rows = own * nz
    half = mentor_unnormalized.shape[0]
    assert rows == n and nc == 2 and PACK % own == 0
    fold = PACK // own
    assert depth % (fold * LANES) == 0
    piece = -(-depth // (fold * nc * LANES)) * LANES
    halves = 2
    assert depth % (halves * LANES) == 0 and depth // (halves * LANES) <= PACK
    wide = -(-vocab // LANES) * LANES
    width = -(-5 * rows // LANES) * LANES
    vmem = pl.BlockSpec(memory_space=pltpu.VMEM)
    hbm = pl.BlockSpec(memory_space=pltpu.HBM)
    dma = pltpu.SemaphoreType.DMA
    results = (
        jax.ShapeDtypeStruct((vocab, depth), jnp.bfloat16),
        jax.ShapeDtypeStruct((1, depth), jnp.bfloat16),
        jax.ShapeDtypeStruct((1, rows), jnp.float32),
    )
    made = pl.pallas_call(
        functools.partial(main_kernel, sizes),
        out_shape=results,
        in_specs=[hbm, hbm, hbm, hbm],
        out_specs=(vmem, vmem, vmem),
        scratch_shapes=[
            pltpu.VMEM((own, depth), jnp.bfloat16),
            pltpu.VMEM(mentor_unnormalized.shape, jnp.float32),
            pltpu.VMEM((1, rows), jnp.int32),
            pltpu.VMEM((vocab, depth), jnp.bfloat16),
            pltpu.VMEM((PACK, piece), jnp.bfloat16),
            pltpu.VMEM((nz, PACK, piece), jnp.bfloat16),
            pltpu.VMEM((nz, PACK, piece), jnp.bfloat16),
            pltpu.VMEM((rows, depth), jnp.bfloat16),
            pltpu.VMEM((half, wide), jnp.float32),
            pltpu.VMEM((half, wide), jnp.float32),
            pltpu.VMEM((1, width), jnp.float32),
            pltpu.VMEM((n, 1, width), jnp.float32),
            pltpu.VMEM((halves, rows * PACK, LANES), jnp.float32),
            pltpu.VMEM((halves, rows // nc, PACK, LANES), jnp.float32),
            pltpu.VMEM((halves, rows // nc, PACK, LANES), jnp.bfloat16),
            pltpu.VMEM((halves, rows // nc, PACK, LANES), jnp.bfloat16),
        ] + [dma] * 11 + [dma((nz,))] + [dma((halves,))] * 4,
        compiler_params=pltpu.CompilerParams(
            collective_id=0, has_side_effects=True, vmem_limit_bytes=44 * 2**20
        ),
    )(*(
        pltpu.with_memory_space_constraint(a, pltpu.HBM)
        for a in (hidden_rows, mentor_unnormalized, head_weight, row_mask.reshape(1, rows))
    ))
    wg, hg, div = pl.pallas_call(
        write_kernel,
        out_shape=results,
        in_specs=[vmem, vmem, vmem],
        out_specs=(hbm, hbm, hbm),
        scratch_shapes=[dma((4,)), dma, dma],
        compiler_params=pltpu.CompilerParams(vmem_limit_bytes=4 * 2**20),
    )(*(pltpu.with_memory_space_constraint(a, pltpu.VMEM) for a in made))
    return div.reshape(rows), hg, wg


def solution(mesh):
    sizes = (mesh.shape["vocab"], mesh.shape["rows"], mesh.shape["teach"])
    return jax.shard_map(
        functools.partial(body, sizes),
        mesh=mesh,
        in_specs=(
            P(("groups", "vocab"), None),
            P(("groups", "teach"), ("vocab", "rows")),
            P(("vocab", "rows", "teach"), None),
            P("groups"),
        ),
        out_specs=(
            P("groups"),
            P(("groups", "vocab", "rows", "teach"), None),
            P(("groups", "vocab", "rows", "teach"), None),
        ),
        check_vma=False,
    )
```

```python
import functools

import jax
import jax.numpy as jnp
from jax import lax
from jax.experimental import pallas as pl
from jax.experimental.pallas import tpu as pltpu
from jax.sharding import PartitionSpec as P

smoothing_divisor = 2.0
objective_scale = 256.0

LANES = 128
PACK = 16


def dot(a, b, contract):
    return lax.dot_general(a, b, ((contract[:1], contract[1:]), ((), ())), preferred_element_type=jnp.float32)


def column_to_row(columns, width):
    rows = columns[0].shape[0]
    lane = lax.broadcasted_iota(jnp.int32, (rows, width), 1)
    row = lax.broadcasted_iota(jnp.int32, (rows, width), 0)
    total = jnp.zeros((rows, width), jnp.float32)
    for place, column in enumerate(columns):
        total = jnp.where(lane == row + place * rows, column, total)
    return jnp.sum(total, axis=0, keepdims=True)


def row_to_column(line, place, rows):
    width = line.shape[1]
    lane = lax.broadcasted_iota(jnp.int32, (rows, width), 1)
    row = lax.broadcasted_iota(jnp.int32, (rows, width), 0)
    return jnp.sum(jnp.where(lane == row + place * rows, line, 0.0), axis=1, keepdims=True)


def partners(index, size):
    if size & (size - 1):
        return [index] + [lax.rem(index + k, size) for k in range(1, size)]
    result = []
    for k in range(size):
        value = index
        for bit in range(size.bit_length() - 1):
            if k >> bit & 1:
                value = value + (1 - 2 * lax.rem(lax.div(index, 1 << bit), 2)) * (1 << bit)
        result.append(value)
    return result


def flipped(index, k, size):
    if size & (size - 1):
        return lax.rem(index + k, size)
    value = index
    for bit in range(size.bit_length() - 1):
        has, flip = (lax.rem(lax.div(v, 1 << bit), 2) for v in (index, k))
        value = value + flip * (1 - 2 * has) * (1 << bit)
    return value


def main_kernel(
    sizes,
    hid_hbm, mentor_hbm, w_hbm, mask_hbm,
    wg, hg, div,
    hid, mentor, mask, w, direct, relayed, h, tsend, trecv, ssend, srecv, part, theirs_part, gsend, grecv,
    hid_sem, mentor_sem, mask_sem, w_sem,
    rs_sem, rr_sem, ts_sem, tr_sem, ss_sem, sr_sem, hr_sem, up_sem, down_sem, ps_sem, pr_sem, gs_sem, gr_sem,
):
    nz, nx, nc = sizes
    n = nz * nx * nc
    own, depth = hid.shape
    rows = own * nz
    vocab = w.shape[0]
    fold = PACK // own
    span = depth // fold
    halves = part.shape[0]
    reach = depth // halves
    unrolled = n <= 16

    z, x, c = lax.axis_index("vocab"), lax.axis_index("rows"), lax.axis_index("teach")
    me = (z * nx + x) * nc + c

    def others(step):
        def run(i, carry):
            d = flipped(me, n - 1 - i, n)
            step(d, {
                "vocab": lax.div(d, nx * nc), "rows": lax.rem(lax.div(d, nc), nx), "teach": lax.rem(d, nc),
            })
            return carry

        lax.fori_loop(0, n - 1, run, 0)

    def same_core(step):
        def run(i, carry):
            d = flipped(z * nx + x, nz * nx - 1 - i, nz * nx)
            step(d, {"vocab": lax.div(d, nx), "rows": lax.rem(d, nx)})
            return carry

        lax.fori_loop(0, nz * nx - 1, run, 0)

    barrier = pltpu.get_barrier_semaphore()

    def greet(at):
        pl.semaphore_signal(barrier, inc=1, device_id=at, device_id_type=pl.DeviceIdType.MESH)

    has_up, has_down = z < nz - 1, z > 0
    pl.when(has_up)(lambda: greet({"vocab": z + 1}))
    pl.when(has_down)(lambda: greet({"vocab": z - 1}))
    for i in range(1, nx * nc):
        greet({"rows": lax.rem(x + i // nc, nx), "teach": lax.rem(c + i % nc, nc)})

    inputs = [
        pltpu.make_async_copy(hid_hbm, hid, hid_sem),
        pltpu.make_async_copy(mentor_hbm, mentor, mentor_sem),
        pltpu.make_async_copy(mask_hbm, mask, mask_sem),
        pltpu.make_async_copy(w_hbm, w, w_sem),
    ]
    for copy in inputs:
        copy.start()

    first = c == 0
    piece = direct.shape[2]
    rest_of = span - piece
    inputs[0].wait()
    hidden = hid[...].astype(jnp.float32)
    packed = jnp.concatenate([hidden[:, k * span:(k + 1) * span] for k in range(fold)], axis=0).astype(jnp.bfloat16)
    low, high = packed[:, :piece], packed[:, rest_of:]
    direct[z] = jnp.where(first, low, high)
    relayed[z] = jnp.where(first, high, low)

    neighbours = jnp.where(has_up, 1, 0) + jnp.where(has_down, 1, 0)
    pl.semaphore_wait(barrier, neighbours + nx * nc - 1)

    def hop(source, up):
        return pltpu.make_async_remote_copy(
            src_ref=direct.at[source], dst_ref=direct.at[source],
            send_sem=(up_sem if up else down_sem).at[source], recv_sem=hr_sem.at[source],
            device_id={"vocab": z + 1 if up else z - 1}, device_id_type=pl.DeviceIdType.MESH,
        )

    pl.when(has_up)(lambda: hop(z, True).start())
    pl.when(has_down)(lambda: hop(z, False).start())

    def receive(source, up):
        pltpu.make_async_copy(direct.at[source], direct.at[source], hr_sem.at[source]).wait()
        pl.when(has_up if up else has_down)(lambda: hop(source, up).start())
        pltpu.make_async_remote_copy(
            src_ref=direct.at[source], dst_ref=relayed.at[source], send_sem=rs_sem, recv_sem=rr_sem,
            device_id={"teach": 1 - c}, device_id_type=pl.DeviceIdType.MESH,
        ).start()

    inputs[1].wait()
    low = mentor[:, :vocab]
    high = mentor[:, vocab:2 * vocab]
    mine = jnp.where(first, low, high)
    tsend[:, :vocab] = jnp.where(first, high, low)
    teacher_copy = pltpu.make_async_remote_copy(
        src_ref=tsend, dst_ref=trecv, send_sem=ts_sem, recv_sem=tr_sem,
        device_id={"teach": 1 - c}, device_id_type=pl.DeviceIdType.MESH,
    )
    teacher_copy.start()
    part[...] = jnp.zeros_like(part)
    inputs[2].wait()
    keep = row_to_column(mask[...].astype(jnp.float32), 0, rows)

    for k in range(1, nz):
        pl.when(z - k >= 0)(lambda k=k: receive(z - k, True))
    for k in range(1, nz):
        pl.when(z + k < nz)(lambda k=k: receive(z + k, False))

    teacher_copy.wait_recv()
    theirs = trecv[:, :vocab]
    scaled = jnp.concatenate(
        [jnp.where(first, mine, theirs), jnp.where(first, theirs, mine)], axis=0
    ) * (1.0 / smoothing_divisor)
    max_t = jnp.max(scaled, axis=1, keepdims=True)
    weight_t = jnp.exp(scaled - max_t)
    sum_t = jnp.sum(weight_t, axis=1, keepdims=True)

    inputs[3].wait()

    def columns_of(held, k, start, width):
        return jnp.concatenate(
            [held[zz, :, pl.ds(start, width)][k * own:(k + 1) * own].astype(jnp.float32) for zz in range(nz)], axis=0
        ).astype(jnp.bfloat16)

    logits = jnp.zeros((rows, vocab), jnp.float32)
    for k in range(fold):
        at = pl.multiple_of(k * span + c * rest_of, LANES)
        logits += dot(columns_of(direct, k, 0, piece), w[:, pl.ds(at, piece)], (1, 1))
    peers = relayed.at[pl.ds(0, nz - 1)]
    pltpu.make_async_copy(peers, peers, rr_sem).wait()
    for k in range(fold):
        start = pl.multiple_of((1 - c) * (piece - rest_of), LANES)
        at = pl.multiple_of(k * span + (1 - c) * piece, LANES)
        logits += dot(columns_of(relayed, k, start, rest_of), w[:, pl.ds(at, rest_of)], (1, 1))

    student = logits * (1.0 / smoothing_divisor)
    max_s = jnp.max(student, axis=1, keepdims=True)
    weight_s = jnp.exp(student - max_s)
    sum_s = jnp.sum(weight_s, axis=1, keepdims=True)
    cross = jnp.sum(weight_t * (scaled - student), axis=1, keepdims=True)

    width = ssend.shape[1]
    line = column_to_row([max_s, max_t, sum_s, sum_t, cross], width)
    ssend[...] = line
    srecv[me] = line
    others(
        lambda d, at: pltpu.make_async_remote_copy(
            src_ref=ssend, dst_ref=srecv.at[me], send_sem=ss_sem, recv_sem=sr_sem,
            device_id=at, device_id_type=pl.DeviceIdType.MESH,
        ).start()
    )
    arrived = []
    for k in range(nz):
        low = jnp.where(first, direct[k], relayed[k])
        high = jnp.where(first, relayed[k], direct[k])
        arrived.append(jnp.concatenate([low, high[:, piece - rest_of:]], axis=1).astype(jnp.float32))
    for k in range(fold):
        h[:, k * span:(k + 1) * span] = jnp.concatenate(
            [a[k * own:(k + 1) * own] for a in arrived], axis=0
        ).astype(jnp.bfloat16)
    pltpu.make_async_copy(srecv.at[pl.ds(0, n - 1)], srecv.at[pl.ds(0, n - 1)], sr_sem).wait()
    stats = srecv[:, 0, :]
    top = jnp.max(stats, axis=0, keepdims=True)
    scale = jnp.exp(stats - top)
    lane = lax.broadcasted_iota(jnp.int32, stats.shape, 1)
    scale = jnp.where(lane < 4 * rows, pltpu.roll(scale, 2 * rows, 1), pltpu.roll(scale, 3 * rows, 1))
    sums = jnp.sum(stats * scale, axis=0, keepdims=True)
    all_max_s, all_max_t = row_to_column(top, 0, rows), row_to_column(top, 1, rows)
    all_sum_s, all_sum_t, all_cross = (row_to_column(sums, k, rows) for k in (2, 3, 4))
    lse_s = all_max_s + jnp.log(all_sum_s)
    lse_t = all_max_t + jnp.log(all_sum_t)

    factor = keep * (objective_scale * smoothing_divisor)
    grad = (
        weight_s * (factor * jnp.exp(max_s - lse_s)) - weight_t * (factor * jnp.exp(max_t - lse_t))
    ).astype(jnp.bfloat16)

    chips = nz * nx
    place = z * nx + x
    swaps = []
    for s in range(halves):
        term = dot(grad, w[:, s * reach:(s + 1) * reach], (1, 0))
        for k in range(reach // LANES):
            part[s, pl.ds(k, rows, stride=PACK), :] = term[:, k * LANES:(k + 1) * LANES]
        swaps.append(pltpu.make_async_remote_copy(
            src_ref=part.at[s].reshape(chips, nc, PACK, LANES).at[:, 1 - c], dst_ref=theirs_part.at[s],
            send_sem=ps_sem.at[s], recv_sem=pr_sem.at[s],
            device_id={"teach": 1 - c}, device_id_type=pl.DeviceIdType.MESH,
        ))
        swaps[-1].start()
    step = depth // 14 if depth % (14 * LANES) == 0 else LANES
    early = depth // step // 5

    grad_t = grad.astype(jnp.float32).T.astype(jnp.bfloat16)

    def weight_grad(i, carry):
        at = pl.ds(pl.multiple_of(i * step, step), step)
        wg[:, at] = dot(grad_t, h[:, at], (1, 0)).astype(jnp.bfloat16)
        return carry

    for s in range(halves):
        lax.fori_loop(s * early, (s + 1) * early, weight_grad, 0)
        swaps[s].wait_recv()
        both = part[s].reshape(chips, nc, PACK, LANES)
        own_part = jnp.where(first, both[:, 0], both[:, 1])
        gsend[s] = (own_part + theirs_part[s]).astype(jnp.bfloat16)
        same_core(
            lambda d, at: pltpu.make_async_remote_copy(
                src_ref=gsend.at[s, d], dst_ref=grecv.at[s, place],
                send_sem=gs_sem.at[s], recv_sem=gr_sem.at[s],
                device_id=at, device_id_type=pl.DeviceIdType.MESH,
            ).start()
        )
        grecv[s, place] = gsend[s, place]

    div[...] = column_to_row([keep * (all_cross / all_sum_t - lse_t + lse_s)], rows)
    lax.fori_loop(halves * early, depth // step, weight_grad, 0)

    for s in range(halves):
        rest = grecv.at[s, pl.ds(0, chips - 1)]
        pltpu.make_async_copy(rest, rest, gr_sem.at[s]).wait()
        total = jnp.sum(grecv[s].astype(jnp.float32), axis=0)
        for k in range(reach // LANES):
            at = s * reach + k * LANES
            hg[:, at:at + LANES] = total[k:k + 1].astype(jnp.bfloat16)

    for k in range(nz):
        pl.when(jnp.logical_and(has_up, k <= z))(lambda k=k: hop(k, True).wait_send())
        pl.when(jnp.logical_and(has_down, k >= z))(lambda k=k: hop(k, False).wait_send())
    pltpu.make_async_copy(peers, peers, rs_sem).wait()
    teacher_copy.wait_send()
    for swap in swaps:
        swap.wait_send()
    pltpu.make_async_copy(srecv.at[pl.ds(0, n - 1)], srecv.at[pl.ds(0, n - 1)], ss_sem).wait()
    for s in range(halves):
        rest = grecv.at[s, pl.ds(0, chips - 1)]
        pltpu.make_async_copy(rest, rest, gs_sem.at[s]).wait()


def write_kernel(wg, hg, div, wg_out, hg_out, div_out, wg_sem, hg_sem, div_sem):
    vocab = wg.shape[0]
    slab = -(-vocab // (wg_sem.shape[0] * PACK)) * PACK
    copies = [pltpu.make_async_copy(hg, hg_out, hg_sem), pltpu.make_async_copy(div, div_out, div_sem)]
    for k, first in enumerate(range(0, vocab, slab)):
        at = pl.ds(first, min(slab, vocab - first))
        copies.append(pltpu.make_async_copy(wg.at[at], wg_out.at[at], wg_sem.at[k]))
    for copy in copies:
        copy.start()
    for copy in copies:
        copy.wait()


def body(sizes, hidden_rows, mentor_unnormalized, head_weight, row_mask):
    nz, nx, nc = sizes
    n = nz * nx * nc
    own, depth = hidden_rows.shape
    vocab = head_weight.shape[0]
    rows = own * nz
    half = mentor_unnormalized.shape[0]
    assert rows == n and nc == 2 and PACK % own == 0
    fold = PACK // own
    assert depth % (fold * LANES) == 0
    piece = -(-depth // (fold * nc * LANES)) * LANES
    halves = 2
    assert depth % (halves * LANES) == 0 and depth // (halves * LANES) <= PACK
    wide = -(-vocab // LANES) * LANES
    width = -(-5 * rows // LANES) * LANES
    vmem = pl.BlockSpec(memory_space=pltpu.VMEM)
    hbm = pl.BlockSpec(memory_space=pltpu.HBM)
    dma = pltpu.SemaphoreType.DMA
    results = (
        jax.ShapeDtypeStruct((vocab, depth), jnp.bfloat16),
        jax.ShapeDtypeStruct((1, depth), jnp.bfloat16),
        jax.ShapeDtypeStruct((1, rows), jnp.float32),
    )
    made = pl.pallas_call(
        functools.partial(main_kernel, sizes),
        out_shape=results,
        in_specs=[hbm, hbm, hbm, hbm],
        out_specs=(vmem, vmem, vmem),
        scratch_shapes=[
            pltpu.VMEM((own, depth), jnp.bfloat16),
            pltpu.VMEM(mentor_unnormalized.shape, jnp.float32),
            pltpu.VMEM((1, rows), jnp.int32),
            pltpu.VMEM((vocab, depth), jnp.bfloat16),
            pltpu.VMEM((nz, PACK, piece), jnp.bfloat16),
            pltpu.VMEM((nz, PACK, piece), jnp.bfloat16),
            pltpu.VMEM((rows, depth), jnp.bfloat16),
            pltpu.VMEM((half, wide), jnp.float32),
            pltpu.VMEM((half, wide), jnp.float32),
            pltpu.VMEM((1, width), jnp.float32),
            pltpu.VMEM((n, 1, width), jnp.float32),
            pltpu.VMEM((halves, rows * PACK, LANES), jnp.float32),
            pltpu.VMEM((halves, rows // nc, PACK, LANES), jnp.float32),
            pltpu.VMEM((halves, rows // nc, PACK, LANES), jnp.bfloat16),
            pltpu.VMEM((halves, rows // nc, PACK, LANES), jnp.bfloat16),
        ] + [dma] * 10 + [dma((nz,))] * 3 + [dma((halves,))] * 4,
        compiler_params=pltpu.CompilerParams(
            collective_id=0, has_side_effects=True, vmem_limit_bytes=44 * 2**20
        ),
    )(*(
        pltpu.with_memory_space_constraint(a, pltpu.HBM)
        for a in (hidden_rows, mentor_unnormalized, head_weight, row_mask.reshape(1, rows))
    ))
    wg, hg, div = pl.pallas_call(
        write_kernel,
        out_shape=results,
        in_specs=[vmem, vmem, vmem],
        out_specs=(hbm, hbm, hbm),
        scratch_shapes=[dma((4,)), dma, dma],
        compiler_params=pltpu.CompilerParams(vmem_limit_bytes=4 * 2**20),
    )(*(pltpu.with_memory_space_constraint(a, pltpu.VMEM) for a in made))
    return div.reshape(rows), hg, wg


def solution(mesh):
    sizes = (mesh.shape["vocab"], mesh.shape["rows"], mesh.shape["teach"])
    return jax.shard_map(
        functools.partial(body, sizes),
        mesh=mesh,
        in_specs=(
            P(("groups", "vocab"), None),
            P(("groups", "teach"), ("vocab", "rows")),
            P(("vocab", "rows", "teach"), None),
            P("groups"),
        ),
        out_specs=(
            P("groups"),
            P(("groups", "vocab", "rows", "teach"), None),
            P(("groups", "vocab", "rows", "teach"), None),
        ),
        check_vma=False,
    )
```

```python
import functools

import jax
import jax.numpy as jnp
from jax import lax
from jax.experimental import pallas as pl
from jax.experimental.pallas import tpu as pltpu
from jax.sharding import PartitionSpec as P

smoothing_divisor = 2.0
objective_scale = 256.0

LANES = 128
PACK = 16


def dot(a, b, contract):
    return lax.dot_general(a, b, ((contract[:1], contract[1:]), ((), ())), preferred_element_type=jnp.float32)


def column_to_row(columns, width):
    rows = columns[0].shape[0]
    lane = lax.broadcasted_iota(jnp.int32, (rows, width), 1)
    row = lax.broadcasted_iota(jnp.int32, (rows, width), 0)
    total = jnp.zeros((rows, width), jnp.float32)
    for place, column in enumerate(columns):
        total = jnp.where(lane == row + place * rows, column, total)
    return jnp.sum(total, axis=0, keepdims=True)


def row_to_column(line, place, rows):
    width = line.shape[1]
    lane = lax.broadcasted_iota(jnp.int32, (rows, width), 1)
    row = lax.broadcasted_iota(jnp.int32, (rows, width), 0)
    return jnp.sum(jnp.where(lane == row + place * rows, line, 0.0), axis=1, keepdims=True)


def partners(index, size):
    if size & (size - 1):
        return [index] + [lax.rem(index + k, size) for k in range(1, size)]
    result = []
    for k in range(size):
        value = index
        for bit in range(size.bit_length() - 1):
            if k >> bit & 1:
                value = value + (1 - 2 * lax.rem(lax.div(index, 1 << bit), 2)) * (1 << bit)
        result.append(value)
    return result


def main_kernel(
    sizes,
    hid_hbm, mentor_hbm, w_hbm, mask_hbm,
    wg, hg, div,
    hid, mentor, mask, w, hsend, direct, h, tsend, trecv, ssend, srecv, part, theirs_part, gsend, grecv,
    hid_sem, mentor_sem, mask_sem, w_sem,
    hs_sem, ts_sem, tr_sem, ss_sem, sr_sem, hr_sem, ps_sem, pr_sem, gs_sem, gr_sem,
):
    nz, nx, nc = sizes
    n = nz * nx * nc
    own, depth = hid.shape
    rows = own * nz
    vocab = w.shape[0]
    fold = PACK // own
    span = depth // fold
    halves = part.shape[0]
    reach = depth // halves
    unrolled = n <= 16

    z, x, c = lax.axis_index("vocab"), lax.axis_index("rows"), lax.axis_index("teach")
    me = (z * nx + x) * nc + c

    def others(step):
        if unrolled:
            zs, xs, cs = partners(z, nz), partners(x, nx), partners(c, nc)
            for i in reversed(range(1, n)):
                zz, xx, cc = zs[i // (nx * nc)], xs[i // nc % nx], cs[i % nc]
                step((zz * nx + xx) * nc + cc, {"vocab": zz, "rows": xx, "teach": cc})
            return

        def run(offset, carry):
            d = lax.rem(me + offset, n)
            step(d, {
                "vocab": lax.div(d, nx * nc), "rows": lax.rem(lax.div(d, nc), nx), "teach": lax.rem(d, nc),
            })
            return carry

        lax.fori_loop(1, n, run, 0)

    def same_core(step):
        if unrolled:
            zs, xs = partners(z, nz), partners(x, nx)
            for i in reversed(range(1, nz * nx)):
                zz, xx = zs[i // nx], xs[i % nx]
                step(zz * nx + xx, {"vocab": zz, "rows": xx})
            return

        def run(offset, carry):
            d = lax.rem(z * nx + x + offset, nz * nx)
            step(d, {"vocab": lax.div(d, nx), "rows": lax.rem(d, nx)})
            return carry

        lax.fori_loop(1, nz * nx, run, 0)

    barrier = pltpu.get_barrier_semaphore()

    def greet(at):
        pl.semaphore_signal(barrier, inc=1, device_id=at, device_id_type=pl.DeviceIdType.MESH)

    def greet_line(offset, carry):
        greet({"vocab": lax.rem(z + offset, nz)})
        return carry

    lax.fori_loop(1, nz, greet_line, 0, unroll=nz <= 4)
    for i in range(1, nx * nc):
        greet({"rows": lax.rem(x + i // nc, nx), "teach": lax.rem(c + i % nc, nc)})

    inputs = [
        pltpu.make_async_copy(hid_hbm, hid, hid_sem),
        pltpu.make_async_copy(mentor_hbm, mentor, mentor_sem),
        pltpu.make_async_copy(mask_hbm, mask, mask_sem),
        pltpu.make_async_copy(w_hbm, w, w_sem),
    ]
    for copy in inputs:
        copy.start()

    first = c == 0
    piece = direct.shape[2]
    inputs[0].wait()
    hidden = hid[...].astype(jnp.float32)
    packed = jnp.concatenate([hidden[:, k * span:(k + 1) * span] for k in range(fold)], axis=0).astype(jnp.bfloat16)
    hsend[...] = packed
    direct[z] = packed

    pl.semaphore_wait(barrier, nz - 1 + nx * nc - 1)

    def send_hidden(to):
        pltpu.make_async_remote_copy(
            src_ref=hsend, dst_ref=direct.at[z], send_sem=hs_sem, recv_sem=hr_sem.at[z],
            device_id={"vocab": to}, device_id_type=pl.DeviceIdType.MESH,
        ).start()

    def relay(source):
        pltpu.make_async_copy(hsend, direct.at[source], hr_sem.at[source]).wait()

    def line(step, far_first):
        if unrolled:
            peers = partners(z, nz)[1:]
            for zz in reversed(peers) if far_first else peers:
                step(zz)
            return

        def run(offset, carry):
            step(lax.rem(z + offset, nz))
            return carry

        lax.fori_loop(1, nz, run, 0)

    line(send_hidden, True)

    inputs[1].wait()
    low = mentor[:, :vocab]
    high = mentor[:, vocab:2 * vocab]
    mine = jnp.where(first, low, high)
    tsend[:, :vocab] = jnp.where(first, high, low)
    teacher_copy = pltpu.make_async_remote_copy(
        src_ref=tsend, dst_ref=trecv, send_sem=ts_sem, recv_sem=tr_sem,
        device_id={"teach": 1 - c}, device_id_type=pl.DeviceIdType.MESH,
    )
    teacher_copy.start()
    part[...] = jnp.zeros_like(part)
    inputs[2].wait()
    keep = row_to_column(mask[...].astype(jnp.float32), 0, rows)

    line(relay, False)

    teacher_copy.wait_recv()
    theirs = trecv[:, :vocab]
    scaled = jnp.concatenate(
        [jnp.where(first, mine, theirs), jnp.where(first, theirs, mine)], axis=0
    ) * (1.0 / smoothing_divisor)
    max_t = jnp.max(scaled, axis=1, keepdims=True)
    weight_t = jnp.exp(scaled - max_t)
    sum_t = jnp.sum(weight_t, axis=1, keepdims=True)

    inputs[3].wait()

    def columns_of(held, k, start, width):
        return jnp.concatenate(
            [held[zz, :, pl.ds(start, width)][k * own:(k + 1) * own].astype(jnp.float32) for zz in range(nz)], axis=0
        ).astype(jnp.bfloat16)

    logits = jnp.zeros((rows, vocab), jnp.float32)
    for k in range(fold):
        at = pl.multiple_of(k * span, LANES)
        logits += dot(columns_of(direct, k, 0, piece), w[:, pl.ds(at, piece)], (1, 1))
    peers = direct.at[pl.ds(0, nz - 1)]
    student = logits * (1.0 / smoothing_divisor)
    max_s = jnp.max(student, axis=1, keepdims=True)
    weight_s = jnp.exp(student - max_s)
    sum_s = jnp.sum(weight_s, axis=1, keepdims=True)
    cross = jnp.sum(weight_t * (scaled - student), axis=1, keepdims=True)

    width = ssend.shape[1]
    line = column_to_row([max_s, max_t, sum_s, sum_t, cross], width)
    ssend[...] = line
    srecv[me] = line
    others(
        lambda d, at: pltpu.make_async_remote_copy(
            src_ref=ssend, dst_ref=srecv.at[me], send_sem=ss_sem, recv_sem=sr_sem,
            device_id=at, device_id_type=pl.DeviceIdType.MESH,
        ).start()
    )
    arrived = []
    for k in range(nz):
        arrived.append(direct[k].astype(jnp.float32))
    for k in range(fold):
        h[:, k * span:(k + 1) * span] = jnp.concatenate(
            [a[k * own:(k + 1) * own] for a in arrived], axis=0
        ).astype(jnp.bfloat16)
    pltpu.make_async_copy(srecv.at[pl.ds(0, n - 1)], srecv.at[pl.ds(0, n - 1)], sr_sem).wait()
    stats = srecv[:, 0, :]
    top = jnp.max(stats, axis=0, keepdims=True)
    scale = jnp.exp(stats - top)
    lane = lax.broadcasted_iota(jnp.int32, stats.shape, 1)
    scale = jnp.where(lane < 4 * rows, pltpu.roll(scale, 2 * rows, 1), pltpu.roll(scale, 3 * rows, 1))
    sums = jnp.sum(stats * scale, axis=0, keepdims=True)
    all_max_s, all_max_t = row_to_column(top, 0, rows), row_to_column(top, 1, rows)
    all_sum_s, all_sum_t, all_cross = (row_to_column(sums, k, rows) for k in (2, 3, 4))
    lse_s = all_max_s + jnp.log(all_sum_s)
    lse_t = all_max_t + jnp.log(all_sum_t)

    factor = keep * (objective_scale * smoothing_divisor)
    grad = (
        weight_s * (factor * jnp.exp(max_s - lse_s)) - weight_t * (factor * jnp.exp(max_t - lse_t))
    ).astype(jnp.bfloat16)

    chips = nz * nx
    place = z * nx + x
    swaps = []
    for s in range(halves):
        term = dot(grad, w[:, s * reach:(s + 1) * reach], (1, 0))
        for k in range(reach // LANES):
            part[s, pl.ds(k, rows, stride=PACK), :] = term[:, k * LANES:(k + 1) * LANES]
        swaps.append(pltpu.make_async_remote_copy(
            src_ref=part.at[s].reshape(chips, nc, PACK, LANES).at[:, 1 - c], dst_ref=theirs_part.at[s],
            send_sem=ps_sem.at[s], recv_sem=pr_sem.at[s],
            device_id={"teach": 1 - c}, device_id_type=pl.DeviceIdType.MESH,
        ))
        swaps[-1].start()
    step = depth // 14 if depth % (14 * LANES) == 0 else LANES
    steps = range(0, depth, step)
    early = len(steps) // 5

    def weight_grad(k):
        wg[:, k:k + step] = dot(grad, h[:, k:k + step], (0, 0)).astype(jnp.bfloat16)

    for s in range(halves):
        for k in steps[s * early:(s + 1) * early]:
            weight_grad(k)
        swaps[s].wait_recv()
        both = part[s].reshape(chips, nc, PACK, LANES)
        own_part = jnp.where(first, both[:, 0], both[:, 1])
        gsend[s] = (own_part + theirs_part[s]).astype(jnp.bfloat16)
        same_core(
            lambda d, at: pltpu.make_async_remote_copy(
                src_ref=gsend.at[s, d], dst_ref=grecv.at[s, place],
                send_sem=gs_sem.at[s], recv_sem=gr_sem.at[s],
                device_id=at, device_id_type=pl.DeviceIdType.MESH,
            ).start()
        )
        grecv[s, place] = gsend[s, place]

    div[...] = column_to_row([keep * (all_cross / all_sum_t - lse_t + lse_s)], rows)
    for k in steps[2 * early:]:
        weight_grad(k)

    for s in range(halves):
        rest = grecv.at[s, pl.ds(0, chips - 1)]
        pltpu.make_async_copy(rest, rest, gr_sem.at[s]).wait()
        total = jnp.sum(grecv[s].astype(jnp.float32), axis=0)
        for k in range(reach // LANES):
            at = s * reach + k * LANES
            hg[:, at:at + LANES] = total[k:k + 1].astype(jnp.bfloat16)

    pltpu.make_async_copy(peers, peers, hs_sem).wait()
    teacher_copy.wait_send()
    for swap in swaps:
        swap.wait_send()
    pltpu.make_async_copy(srecv.at[pl.ds(0, n - 1)], srecv.at[pl.ds(0, n - 1)], ss_sem).wait()
    for s in range(halves):
        rest = grecv.at[s, pl.ds(0, chips - 1)]
        pltpu.make_async_copy(rest, rest, gs_sem.at[s]).wait()


def write_kernel(wg, hg, div, wg_out, hg_out, div_out, wg_sem, hg_sem, div_sem):
    vocab = wg.shape[0]
    slab = -(-vocab // (wg_sem.shape[0] * PACK)) * PACK
    copies = [pltpu.make_async_copy(hg, hg_out, hg_sem), pltpu.make_async_copy(div, div_out, div_sem)]
    for k, first in enumerate(range(0, vocab, slab)):
        at = pl.ds(first, min(slab, vocab - first))
        copies.append(pltpu.make_async_copy(wg.at[at], wg_out.at[at], wg_sem.at[k]))
    for copy in copies:
        copy.start()
    for copy in copies:
        copy.wait()


def body(sizes, hidden_rows, mentor_unnormalized, head_weight, row_mask):
    nz, nx, nc = sizes
    n = nz * nx * nc
    own, depth = hidden_rows.shape
    vocab = head_weight.shape[0]
    rows = own * nz
    half = mentor_unnormalized.shape[0]
    assert rows == n and nc == 2 and PACK % own == 0
    fold = PACK // own
    assert depth % (fold * LANES) == 0
    piece = depth // fold
    halves = 2
    assert depth % (halves * LANES) == 0 and depth // (halves * LANES) <= PACK
    wide = -(-vocab // LANES) * LANES
    width = -(-5 * rows // LANES) * LANES
    vmem = pl.BlockSpec(memory_space=pltpu.VMEM)
    hbm = pl.BlockSpec(memory_space=pltpu.HBM)
    dma = pltpu.SemaphoreType.DMA
    results = (
        jax.ShapeDtypeStruct((vocab, depth), jnp.bfloat16),
        jax.ShapeDtypeStruct((1, depth), jnp.bfloat16),
        jax.ShapeDtypeStruct((1, rows), jnp.float32),
    )
    made = pl.pallas_call(
        functools.partial(main_kernel, sizes),
        out_shape=results,
        in_specs=[hbm, hbm, hbm, hbm],
        out_specs=(vmem, vmem, vmem),
        scratch_shapes=[
            pltpu.VMEM((own, depth), jnp.bfloat16),
            pltpu.VMEM(mentor_unnormalized.shape, jnp.float32),
            pltpu.VMEM((1, rows), jnp.int32),
            pltpu.VMEM((vocab, depth), jnp.bfloat16),
            pltpu.VMEM((PACK, piece), jnp.bfloat16),
            pltpu.VMEM((nz, PACK, piece), jnp.bfloat16),
            pltpu.VMEM((rows, depth), jnp.bfloat16),
            pltpu.VMEM((half, wide), jnp.float32),
            pltpu.VMEM((half, wide), jnp.float32),
            pltpu.VMEM((1, width), jnp.float32),
            pltpu.VMEM((n, 1, width), jnp.float32),
            pltpu.VMEM((halves, rows * PACK, LANES), jnp.float32),
            pltpu.VMEM((halves, rows // nc, PACK, LANES), jnp.float32),
            pltpu.VMEM((halves, rows // nc, PACK, LANES), jnp.bfloat16),
            pltpu.VMEM((halves, rows // nc, PACK, LANES), jnp.bfloat16),
        ] + [dma] * 9 + [dma((nz,))] + [dma((halves,))] * 4,
        compiler_params=pltpu.CompilerParams(
            collective_id=0, has_side_effects=True, vmem_limit_bytes=44 * 2**20
        ),
    )(*(
        pltpu.with_memory_space_constraint(a, pltpu.HBM)
        for a in (hidden_rows, mentor_unnormalized, head_weight, row_mask.reshape(1, rows))
    ))
    wg, hg, div = pl.pallas_call(
        write_kernel,
        out_shape=results,
        in_specs=[vmem, vmem, vmem],
        out_specs=(hbm, hbm, hbm),
        scratch_shapes=[dma((4,)), dma, dma],
        compiler_params=pltpu.CompilerParams(vmem_limit_bytes=4 * 2**20),
    )(*(pltpu.with_memory_space_constraint(a, pltpu.VMEM) for a in made))
    return div.reshape(rows), hg, wg


def solution(mesh):
    sizes = (mesh.shape["vocab"], mesh.shape["rows"], mesh.shape["teach"])
    return jax.shard_map(
        functools.partial(body, sizes),
        mesh=mesh,
        in_specs=(
            P(("groups", "vocab"), None),
            P(("groups", "teach"), ("vocab", "rows")),
            P(("vocab", "rows", "teach"), None),
            P("groups"),
        ),
        out_specs=(
            P("groups"),
            P(("groups", "vocab", "rows", "teach"), None),
            P(("groups", "vocab", "rows", "teach"), None),
        ),
        check_vma=False,
    )
```
